512 devices in a mesh: seq: 8 (over y_hi, x), expert: 64 (over z, y_lo, core).
Axes of the slice: x: 4, y: 8 (y_hi: 2, y_lo: 4; y = y_hi * 4 + y_lo), z: 8, core: 2. Of those that a mesh axis runs over, the one named last changes fastest.
Arguments:
- hidden_in: bfloat16 [3072, 4096], P('seq', 'expert'), may hold values from -6 to 6
- queries: bfloat16 [3072, 8192], P('seq', 'expert'), may hold values from -150 to 150
- frame_keys: bfloat16 [24, 201, 1024], P('seq'), may hold values from -6 to 6
- frame_values: bfloat16 [24, 201, 1024], P('seq'), may hold values from -6 to 6
- cited_frame: int32 [3072], P('seq'), may hold values from 0 to 23, as said below
- frame_slot: int32 [24], replicated, may hold values from 0 to 23, as said below
- attn_gate: float32 [4096], P('expert'), may hold values from 0.3 to 2
- out_weight: bfloat16 [8192, 4096], P(None, 'expert'), may hold values from -0.0625 to 0.0625
- mlp_gain: float32 [4096], replicated, may hold values from 0.1 to 1.9
- expert_ids: int32 [3072, 2], P('seq'), may hold values from 0 to 63, all different within a row; in each aligned block of 384 rows (0 to 383, 384 to 767, ...) at most 36 rows name the same one
- gate_fixed: int32 [3072, 2], P('seq'), may hold values from 6554 to 65535
- w_in: bfloat16 [64, 4096, 2, 1024], P('expert', None, None, 'seq'), may hold values from -0.09375 to 0.09375
- w_down: bfloat16 [64, 1024, 4096], P('expert', 'seq'), may hold values from -0.1875 to 0.1875
Outputs:
- hidden_out: bfloat16 [3072, 4096], P('seq', 'expert')
The draws below stay inside these ranges and needn't reach their ends.
Inputs may be any that keep to these rules, and one draw needn't show every extreme that they name: `cited_frame`: any token may cite any frame. `frame_slot`: A permutation of the frame ids. `expert_ids`: the two experts of a token differ; among the 384 tokens of one seq shard no expert is named more than 36 times.
All inputs are finite; a program needn't handle non-finite values.
Results may differ from the reference program's by a relative error of at most 0.015.
Values may be sent and summed in bfloat16 or wider, within the bound.
No kernel may reach another device: no remote copies, remote signals or barrier semaphores. Data moves between devices by JAX's collectives and lax.ppermute only.
A program may use at most 64 MiB of HBM per device.

```python
import math
import jax
import jax.numpy as jnp
import numpy as np
from jax import lax

D = 4096
HD = 128
KVH = 8
TOPK = 2
FFE = 1024
FROWS = 201
TSEQ = 384
HEADS = 64
EXPERTS = 64
FF_DEV = 128
CAP = 36
TOKENS = 3072
FRAMES = 24
N_SEQ = 8


def shared_tables(key):
    cited_ids = jax.random.randint(jax.random.fold_in(key, 101), (TOKENS,), 0, FRAMES, dtype=jnp.int32)
    cited_ids = cited_ids.at[0].set(0).at[TOKENS - 1].set(FRAMES - 1)
    slot_table = jax.random.permutation(jax.random.fold_in(key, 102), FRAMES).astype(jnp.int32)
    key_table = jnp.clip(jax.random.normal(jax.random.fold_in(key, 103), (FRAMES, FROWS, KVH * HD), jnp.float32), -6.0, 6.0)
    return (cited_ids, slot_table, key_table)


def draw_frame_keys(key, part):
    cited_ids, slot_table, key_table = shared_tables(key)
    return key_table.astype(jnp.bfloat16)


def draw_queries(key, part):
    key = jax.random.fold_in(key, 2)
    drawn = jnp.clip(jax.random.normal(key, (TOKENS, HEADS * HD), jnp.float32), -6.0, 6.0)
    return drawn.astype(jnp.bfloat16)


def draw_cited_frame(key, part):
    cited_ids, slot_table, key_table = shared_tables(key)
    return cited_ids


def draw_frame_slot(key, part):
    cited_ids, slot_table, key_table = shared_tables(key)
    return slot_table


def touch_ends(array, rng, least, top_value):
    longest = array.shape.index(max(array.shape))
    spots = []
    for shift in (0, 1):
        where = [jax.random.randint(jax.random.fold_in(rng, axis), (), 0, length) for axis, length in enumerate(array.shape)]
        where[longest] = (where[longest] + shift) % array.shape[longest]
        spots.append(tuple(where))
    return array.at[spots[0]].set(least).at[spots[1]].set(top_value)


def steps_of(stream_key, extent, split, least, high):
    level = 1.0
    for axis_at, blocks in split:
        heights = jax.random.uniform(jax.random.fold_in(jax.random.fold_in(stream_key, 6), axis_at), (blocks,), jnp.float32, least / len(split), high / len(split))
        level = level * jnp.repeat(jnp.exp(heights), extent[axis_at] // blocks).reshape((-1,) + (1,) * (len(extent) - 1 - axis_at))
    return level


def deal_out(own_key, own, number, rows, number_of, top, limit, lean):
    sequence = jax.random.permutation(own_key, number_of)
    packed, common = shares(number_of, rows * top, limit, lean, True), shares(number_of, rows * top, limit, lean, False)
    places = jnp.arange(number_of)

    def named(tallies, turn):
        used = int((tallies > 0).sum())
        fixed = max(1, used // 4)
        passed = fixed + (places - fixed + turn * (used - fixed)) % max(1, number_of - fixed)
        return jnp.zeros((number_of,), jnp.int32).at[sequence[jnp.where(places < fixed, places, passed)]].set(jnp.asarray(tallies, jnp.int32))

    tallies = jnp.where(number % 4 == 0, named(packed, number // 4), named(common, number - number // 4 - 1))
    mixed = jax.random.permutation(jax.random.fold_in(own, 3), number_of)
    source_of, receiver = mixed[0:number_of // 2 * 2:2], mixed[1:number_of // 2 * 2:2]
    slack = jnp.minimum(tallies[source_of] - 1, limit - tallies[receiver]) // 2
    slack = jnp.where((source_of == sequence[0]) | (receiver == sequence[0]) | (tallies[receiver] == 0), 0, jnp.maximum(slack, 0))
    passed = jax.random.randint(jax.random.fold_in(own, 4), (number_of // 2,), 0, 1 << 20) % (slack + 1)
    tallies = tallies.at[source_of].add(-passed).at[receiver].add(passed)
    members = jnp.searchsorted(jnp.cumsum(tallies), jnp.arange(rows * top), side="right").astype(jnp.int32)
    listing = members.reshape(top, rows).T
    listing = listing[jax.random.permutation(jax.random.fold_in(own, 1), rows)]
    turn = jax.random.randint(jax.random.fold_in(own, 2), (rows, 1), 0, top)
    return jnp.take_along_axis(listing, (jnp.arange(top)[None, :] + turn) % top, axis=1)


def shares(amount, total, most, lean, full):
    portions = [(1 << 20) // math.isqrt(standing ** lean) + 1 for standing in range(1, amount + 1)]
    largest = most if full else min(most, max(-(-total // amount), total * portions[0] // sum(portions)))
    least = 1 if total - largest >= amount - 1 else 0
    holding, spare = [largest] + [least] * (amount - 1), total - largest - least * (amount - 1)
    while spare > 0:
        candidates = [i for i in range(1, amount) if holding[i] < largest] or [i for i in range(1, amount) if holding[i] < most]
        mass, left = sum([portions[i] for i in candidates]), spare
        for i in candidates:
            extra = min(most - holding[i], max(1, left * portions[i] // mass), spare)
            holding[i] = holding[i] + extra
            spare = spare - extra
    return np.array(holding)


def bell_draw(own_key, dims, deviation, reach, shards=(), held_as=jnp.bfloat16):
    values = jax.random.normal(own_key, dims, jnp.float32) * deviation
    if len(shards) > 0:
        values = steps_of(own_key, dims, shards, -0.22, 0.18) * values
    return jnp.clip(values, min=-reach, max=reach).astype(held_as)


def setup_inputs(seed: int = 0) -> dict:
    seeds = jax.random.split(jax.random.key(seed), 14)
    hidden_in = bell_draw(seeds[0], (TOKENS, D), 1.0, 6.0, ((0, 8), (1, 64)))
    queries = draw_queries(jax.random.fold_in(seeds[13], 71), 0)
    frame_keys = draw_frame_keys(jax.random.fold_in(seeds[13], 71), 0)
    frame_values = bell_draw(seeds[3], (FRAMES, FROWS, KVH * HD), 1.0, 6.0, ((0, 8),))
    cited_frame = draw_cited_frame(jax.random.fold_in(seeds[13], 71), 0)
    frame_slot = draw_frame_slot(jax.random.fold_in(seeds[13], 71), 0)
    attn_gate = jnp.clip(0.3 + 1.7 * jax.random.uniform(seeds[6], (D,), jnp.float32) ** steps_of(seeds[6], (D,), ((0, 64),), -0.2, 0.2), 0.3, 2.0)
    out_weight = bell_draw(seeds[7], (HEADS * HD, D), (HEADS * HD) ** -0.5, 0.0625, ((1, 64),))
    mlp_gain = jnp.clip(1.0 + 0.18 * jax.random.normal(seeds[8], (D,), jnp.float32), 0.1, 1.9)
    expert_ids_keys = jax.random.split(jax.random.fold_in(seeds[9], 1), TOKENS // TSEQ)
    expert_ids_turns = jax.random.permutation(jax.random.fold_in(seeds[9], 3), TOKENS // TSEQ)
    expert_ids = jax.vmap(lambda own, number: deal_out(jax.random.fold_in(seeds[9], 2), own, number, TSEQ, EXPERTS, TOPK, CAP, 2))(expert_ids_keys, expert_ids_turns).reshape((TOKENS, TOPK))
    gate_fixed = touch_ends(jax.random.randint(seeds[10], (TOKENS, TOPK), 6554, 65536), jax.random.fold_in(seeds[10], 1), 6554, 65535).astype(jnp.int32)
    w_in = bell_draw(seeds[11], (EXPERTS, D, 2, FFE), D ** -0.5, 0.09375, ((0, 64), (3, 8)))
    w_down = bell_draw(seeds[12], (EXPERTS, FFE, D), FFE ** -0.5, 0.1875, ((0, 64), (1, 8)))
    return {"hidden_in": hidden_in, "queries": queries, "frame_keys": frame_keys, "frame_values": frame_values, "cited_frame": cited_frame, "frame_slot": frame_slot, "attn_gate": attn_gate, "out_weight": out_weight, "mlp_gain": mlp_gain, "expert_ids": expert_ids, "gate_fixed": gate_fixed, "w_in": w_in, "w_down": w_down}


FIXED_SCALE = 1.0 / 65536.0
NORM_EPSILON = 1e-05

def rms_normed(rows, gain):
    wide = rows.astype(jnp.float32)
    mean_square = lax.optimization_barrier(jnp.mean(wide * wide, axis=1, keepdims=True))
    return (wide * lax.rsqrt(mean_square + NORM_EPSILON) * gain).astype(jnp.bfloat16)

def reference(hidden_in, queries, frame_keys, frame_values, cited_frame, frame_slot, attn_gate, out_weight, mlp_gain, expert_ids, gate_fixed, w_in, w_down):
    group_size = HEADS // KVH
    score_scale = 1.0 / math.sqrt(HD)
    token_slot = frame_slot[cited_frame]

    def attend_block(operands):
        query_rows, slot_rows = operands
        row_count = query_rows.shape[0]
        key_rows = frame_keys[slot_rows].reshape(row_count, FROWS, KVH, HD).astype(jnp.float32)
        value_rows = frame_values[slot_rows].reshape(row_count, FROWS, KVH, HD).astype(jnp.float32)
        query_heads = query_rows.reshape(row_count, KVH, group_size, HD).astype(jnp.float32)
        scores = jnp.einsum('tgzd,tjgd->tgzj', query_heads, key_rows) * score_scale
        probability = jax.nn.softmax(scores, axis=-1).astype(jnp.bfloat16)
        mixed = jnp.einsum('tgzj,tjgd->tgzd', probability.astype(jnp.float32), value_rows)
        return mixed.reshape(row_count, HEADS * HD).astype(jnp.bfloat16)
    attended = lax.map(attend_block, (queries.reshape(N_SEQ, TSEQ, HEADS * HD), token_slot.reshape(N_SEQ, TSEQ)))
    attended = attended.reshape(TOKENS, HEADS * HD)
    projected = jnp.dot(attended, out_weight, preferred_element_type=jnp.float32)
    mid = (hidden_in.astype(jnp.float32) + jnp.tanh(attn_gate)[None, :] * projected).astype(jnp.bfloat16)
    normed = rms_normed(mid, mlp_gain)
    shard_ids = expert_ids.reshape(N_SEQ, TSEQ * TOPK)
    expert_cols = jnp.arange(EXPERTS, dtype=jnp.int32)
    matches = (shard_ids[:, :, None] == expert_cols[None, None, :]).astype(jnp.int32)
    rank_of = lax.optimization_barrier(jnp.sum(jnp.cumsum(matches, axis=1) * matches, axis=2)) - 1
    shard_index = jnp.arange(N_SEQ, dtype=jnp.int32)[:, None]
    slot_of = (shard_ids * N_SEQ + shard_index) * CAP + rank_of
    token_of = shard_index * TSEQ + jnp.arange(TSEQ * TOPK, dtype=jnp.int32)[None, :] // TOPK
    table = jnp.zeros((EXPERTS * N_SEQ * CAP,), jnp.int32).at[slot_of.reshape(-1)].set(token_of.reshape(-1) + 1)
    padded = jnp.concatenate([jnp.zeros((1, D), jnp.bfloat16), normed], axis=0)
    expert_rows = padded[table].reshape(EXPERTS, N_SEQ * CAP, D)

    def run_expert(operands):
        rows_in, weight_in, weight_down = operands
        gate_up = jnp.dot(rows_in, weight_in.reshape(D, 2 * FFE), preferred_element_type=jnp.float32)
        activated = (jax.nn.silu(gate_up[:, :FFE]) * gate_up[:, FFE:]).astype(jnp.bfloat16)
        running_sum = jnp.zeros((rows_in.shape[0], D), jnp.float32)
        for block_index in range(FFE // FF_DEV):
            lower = block_index * FF_DEV
            partial_sum = jnp.dot(activated[:, lower:lower + FF_DEV], weight_down[lower:lower + FF_DEV], preferred_element_type=jnp.float32)
            running_sum = running_sum + lax.optimization_barrier(partial_sum.astype(jnp.bfloat16)).astype(jnp.float32)
        return running_sum.astype(jnp.bfloat16)
    expert_out = lax.map(run_expert, (expert_rows, w_in, w_down)).reshape(-1, D)
    picked = expert_out[slot_of.reshape(-1)].astype(jnp.float32).reshape(TOKENS, TOPK, D)
    weights = gate_fixed.astype(jnp.float32) * FIXED_SCALE
    combined = lax.optimization_barrier(jnp.sum(picked * weights[:, :, None], axis=1))
    return (mid.astype(jnp.float32) + combined).astype(jnp.bfloat16)
```

```python
import math

import jax
import jax.numpy as jnp
from jax import lax
from jax.sharding import Mesh
from jax.sharding import PartitionSpec as P

FIXED_SCALE = 1.0 / 65536.0
NORM_EPSILON = 1e-05
MASKED_SCORE = -1e30
SEQ = ("yh", "x")
EXP = ("z", "yl", "core")
NEAR = ("yl", "core")
f32, bf16 = jnp.float32, jnp.bfloat16


def swap(v, axis):
    return lax.ppermute(v, axis, [(0, 1), (1, 0)])


def spread(v, axis):
    n = lax.axis_size(axis)
    return lax.all_to_all(jnp.broadcast_to(v[None], (n,) + v.shape), axis, 0, 0, tiled=True)


def route_tables(expert_ids, gate_fixed, experts, capacity):
    token_count, top_count = expert_ids.shape
    flat_ids = expert_ids.reshape(-1)
    assigned = flat_ids.shape[0]
    expert_cols = lax.broadcasted_iota(jnp.int32, (assigned, experts), 1)
    matches = flat_ids[:, None] == expert_cols
    before = lax.broadcasted_iota(jnp.int32, (assigned, assigned), 1) < lax.broadcasted_iota(
        jnp.int32, (assigned, assigned), 0
    )
    counts = jnp.dot(before.astype(bf16), matches.astype(bf16), preferred_element_type=f32)
    rank_of = jnp.sum(jnp.where(matches, counts, 0.0), axis=1).astype(jnp.int32)
    slot_of = (flat_ids * capacity + rank_of).reshape(token_count, top_count)
    slot_cols = lax.broadcasted_iota(jnp.int32, (token_count, experts * capacity), 1)
    selectors = [(slot_of[:, k : k + 1] == slot_cols) for k in range(top_count)]
    weights = gate_fixed.astype(f32) * FIXED_SCALE
    return selectors, weights


def attention(queries, keys, values, slot, frame_ids, frame_rows):
    width = keys.shape[0]
    scale = 1.0 / math.sqrt(queries.shape[1])
    scores = lax.dot_general(queries, keys, (((1,), (1,)), ((), ())), preferred_element_type=f32) * scale
    column_frame = jnp.repeat(frame_ids, frame_rows, total_repeat_length=width)
    inside = column_frame[None, :] == slot[:, None]
    scores = jnp.where(inside, scores, MASKED_SCORE)
    row_max = jnp.max(scores, axis=1, keepdims=True)
    expon = jnp.exp(scores - row_max)
    row_total = jnp.sum(expon, axis=1, keepdims=True)
    probability = (expon / row_total).astype(bf16)
    mixed = jnp.dot(probability, values, preferred_element_type=f32)
    present = jnp.any(frame_ids[None, :] == slot[:, None], axis=1, keepdims=True)
    return jnp.where(present, mixed, 0.0).astype(bf16)


def per_device(
    hidden_in,
    queries,
    frame_keys,
    frame_values,
    cited_frame,
    frame_slot,
    attn_gate,
    out_weight,
    mlp_gain,
    expert_ids,
    gate_fixed,
    w_in,
    w_down,
):
    head = queries.shape[1]
    tokens = queries.shape[0]
    nx, nz, nh = lax.axis_size("x"), lax.axis_size("z"), lax.axis_size("yh")
    experts = lax.axis_size(EXP)
    near = lax.axis_size(NEAR)
    feats = hidden_in.shape[1]
    yh, x, z = lax.axis_index("yh"), lax.axis_index("x"), lax.axis_index("z")
    held, frame_rows = frame_keys.shape[0], frame_keys.shape[1]
    own = jnp.concatenate(
        [
            lax.dynamic_slice_in_dim(frame_keys, z * head, head, 2).reshape(held * frame_rows, head),
            lax.dynamic_slice_in_dim(frame_values, z * head, head, 2).reshape(held * frame_rows, head),
        ],
        axis=0,
    )
    other = swap(own, "yh")
    half = held * frame_rows
    keys = jnp.concatenate([own[:half], other[:half]], axis=0)
    values = jnp.concatenate([own[half:], other[half:]], axis=0)
    turned = out_weight.T.reshape(feats, nz, near * head).transpose(1, 0, 2)
    near_weight = lax.all_to_all(turned, "z", 0, 0, tiled=True).reshape(nz * feats, near * head)
    frame_cols = lax.broadcasted_iota(jnp.int32, (tokens, frame_slot.shape[0]), 1)
    token_slot = jnp.sum(jnp.where(cited_frame[:, None] == frame_cols, frame_slot[None, :], 0), axis=1)
    slot_rows = jnp.zeros((16, head), bf16).at[: tokens // head].set(
        token_slot.reshape(tokens // head, head).astype(bf16)
    )
    gathered = spread(jnp.concatenate([queries, slot_rows]), "x")
    all_queries = gathered[:, :tokens].reshape(nx * tokens, head)
    all_slots = gathered[:, tokens : tokens + tokens // head].reshape(nx * tokens).astype(jnp.int32)
    frame_ids = jnp.concatenate(
        [held * (h * nx + x) + jnp.arange(held, dtype=jnp.int32) for h in (yh, 1 - yh)]
    )
    mixed = attention(all_queries, keys, values, all_slots, frame_ids, frame_rows)
    back = lax.all_to_all(mixed.reshape(nx, tokens, head), "x", 0, 0, tiled=True)
    attended = jnp.sum(back.astype(f32), axis=0).astype(bf16)
    heads = lax.all_gather(attended, NEAR, axis=1, tiled=True)
    partial = lax.dot_general(
        near_weight, heads, (((1,), (1,)), ((), ())), preferred_element_type=f32
    ).astype(bf16)
    parts = lax.all_to_all(partial.reshape(nz, feats, tokens), "z", 0, 0, tiled=True)
    projected = jnp.sum(parts.astype(f32), axis=0)
    mid = (hidden_in.T.astype(f32) + jnp.tanh(attn_gate)[:, None] * projected).astype(bf16)
    capacity = 6 * tokens // experts
    selectors, weights = route_tables(expert_ids, gate_fixed, experts, capacity)
    select_rows = (selectors[0] | selectors[1]).astype(bf16)
    sent = lax.dot_general(
        select_rows, mid, (((0,), (1,)), ((), ())), preferred_element_type=f32
    ).astype(bf16)
    came = lax.all_to_all(sent.reshape(experts, capacity, feats), EXP, 0, 0, tiled=True)
    rows = came.transpose(1, 0, 2).reshape(capacity, experts * feats)
    wide = rows.astype(f32)
    mean_square = jnp.mean(wide * wide, axis=1, keepdims=True)
    normed = (wide * lax.rsqrt(mean_square + NORM_EPSILON) * mlp_gain).astype(bf16)
    far = swap(normed, "yh")
    pair = jnp.where(yh == 0, jnp.concatenate([normed, far]), jnp.concatenate([far, normed]))
    everyone = spread(pair, "x").reshape(nx * nh * capacity, experts * feats)
    hidden_units = w_in.shape[3]
    expert_in = w_in[0].reshape(w_in.shape[1], 2 * hidden_units)
    gate_up = jnp.dot(everyone, expert_in, preferred_element_type=f32)
    activated = (jax.nn.silu(gate_up[:, :hidden_units]) * gate_up[:, hidden_units:]).astype(bf16)
    down = jnp.dot(activated, w_down[0], preferred_element_type=f32).astype(bf16)
    over_x = lax.all_to_all(
        down.reshape(nx, nh * capacity, experts * feats), "x", 0, 0, tiled=True
    )
    halves = jnp.sum(over_x.astype(f32), axis=0)
    low, high = halves[:capacity], halves[capacity:]
    mine, theirs = jnp.where(yh == 0, low, high), jnp.where(yh == 0, high, low)
    summed = (mine + swap(theirs.astype(bf16), "yh").astype(f32)).astype(bf16)
    dealt = summed.reshape(capacity, experts, feats).transpose(1, 0, 2)
    came_back = lax.all_to_all(dealt, EXP, 0, 0, tiled=True).reshape(experts * capacity, feats)
    mixed_out = sum(
        jnp.dot(s.astype(bf16), came_back, preferred_element_type=f32) * weights[:, k : k + 1]
        for k, s in enumerate(selectors)
    )
    return (mid.T.astype(f32) + mixed_out).astype(bf16)


def solution(mesh):
    fine = Mesh(mesh.devices.reshape(2, 4, 8, 4, 2), SEQ + EXP)
    return jax.shard_map(
        per_device,
        mesh=fine,
        in_specs=(
            P(SEQ, EXP),
            P(SEQ, EXP),
            P(SEQ, None, None),
            P(SEQ, None, None),
            P(SEQ),
            P(),
            P(EXP),
            P(None, EXP),
            P(),
            P(SEQ, None),
            P(SEQ, None),
            P(EXP, None, None, SEQ),
            P(EXP, SEQ, None),
        ),
        out_specs=P(SEQ, EXP),
        check_vma=False,
    )
```

```python
import math

import jax
import jax.numpy as jnp
from jax import lax
from jax.sharding import Mesh
from jax.sharding import PartitionSpec as P

FIXED_SCALE = 1.0 / 65536.0
NORM_EPSILON = 1e-05
MASKED_SCORE = -1e30
SEQ = ("yh", "x")
EXP = ("z", "yl", "core")
NEAR = ("yl", "core")
BOTH = ("yh",) + EXP
f32, bf16 = jnp.float32, jnp.bfloat16


def swap(v, axis):
    return lax.ppermute(v, axis, [(0, 1), (1, 0)])


def shift(v, axis, by):
    n = lax.axis_size(axis)
    return lax.ppermute(v, axis, [(i, (i + by) % n) for i in range(n)])


def tie(*values):
    return lax.optimization_barrier(values)


def spread(v, axis):
    n = lax.axis_size(axis)
    return lax.all_to_all(jnp.broadcast_to(v[None], (n,) + v.shape), axis, 0, 0, tiled=True)


def route_tables(expert_ids, gate_fixed, experts, capacity):
    token_count, top_count = expert_ids.shape
    flat_ids = expert_ids.reshape(-1)
    assigned = flat_ids.shape[0]
    expert_cols = lax.broadcasted_iota(jnp.int32, (assigned, experts), 1)
    matches = flat_ids[:, None] == expert_cols
    before = lax.broadcasted_iota(jnp.int32, (assigned, assigned), 1) < lax.broadcasted_iota(
        jnp.int32, (assigned, assigned), 0
    )
    counts = jnp.dot(before.astype(bf16), matches.astype(bf16), preferred_element_type=f32)
    rank_of = jnp.sum(jnp.where(matches, counts, 0.0), axis=1).astype(jnp.int32)
    slot_of = (flat_ids * capacity + rank_of).reshape(token_count, top_count)
    slot_cols = lax.broadcasted_iota(jnp.int32, (token_count, experts * capacity), 1)
    selectors = [(slot_of[:, k : k + 1] == slot_cols) for k in range(top_count)]
    weights = gate_fixed.astype(f32) * FIXED_SCALE
    return selectors, weights


def attention(queries, keys, values, slot, frame_ids, frame_rows):
    width = keys.shape[0]
    scale = 1.0 / math.sqrt(queries.shape[1])
    scores = lax.dot_general(queries, keys, (((1,), (1,)), ((), ())), preferred_element_type=f32) * scale
    column_frame = jnp.repeat(frame_ids, frame_rows, total_repeat_length=width)
    inside = column_frame[None, :] == slot[:, None]
    scores = jnp.where(inside, scores, MASKED_SCORE)
    row_max = jnp.max(scores, axis=1, keepdims=True)
    expon = jnp.exp(scores - row_max)
    row_total = jnp.sum(expon, axis=1, keepdims=True)
    probability = (expon / row_total).astype(bf16)
    mixed = jnp.dot(probability, values, preferred_element_type=f32)
    present = jnp.any(frame_ids[None, :] == slot[:, None], axis=1, keepdims=True)
    return jnp.where(present, mixed, 0.0).astype(bf16)


def per_device(
    hidden_in,
    queries,
    frame_keys,
    frame_values,
    cited_frame,
    frame_slot,
    attn_gate,
    out_weight,
    mlp_gain,
    expert_ids,
    gate_fixed,
    w_in,
    w_down,
):
    head = queries.shape[1]
    tokens = queries.shape[0]
    nx, nz, nh = lax.axis_size("x"), lax.axis_size("z"), lax.axis_size("yh")
    experts = lax.axis_size(EXP)
    near = lax.axis_size(NEAR)
    feats = hidden_in.shape[1]
    yh, x, z = lax.axis_index("yh"), lax.axis_index("x"), lax.axis_index("z")
    held, frame_rows = frame_keys.shape[0], frame_keys.shape[1]
    in_left, in_right = shift(w_in[0], "x", 1), shift(w_in[0], "x", -1)
    down_left, down_right = shift(w_down[0], "x", 1), shift(w_down[0], "x", -1)
    own = jnp.concatenate(
        [
            lax.dynamic_slice_in_dim(frame_keys, z * head, head, 2).reshape(held * frame_rows, head),
            lax.dynamic_slice_in_dim(frame_values, z * head, head, 2).reshape(held * frame_rows, head),
        ],
        axis=0,
    )
    other = swap(own, "yh")
    half = held * frame_rows
    keys = jnp.concatenate([own[:half], other[:half]], axis=0)
    values = jnp.concatenate([own[half:], other[half:]], axis=0)
    frame_cols = lax.broadcasted_iota(jnp.int32, (tokens, frame_slot.shape[0]), 1)
    token_slot = jnp.sum(jnp.where(cited_frame[:, None] == frame_cols, frame_slot[None, :], 0), axis=1)
    slot_rows = jnp.zeros((16, head), bf16).at[: tokens // head].set(
        token_slot.reshape(tokens // head, head).astype(bf16)
    )
    packed = jnp.concatenate([queries, slot_rows])
    gathered = spread(packed, "x")
    gathered, turned = tie(gathered, out_weight.T)
    turned = turned.reshape(feats, nz, near * head).transpose(1, 0, 2)
    near_weight = lax.all_to_all(turned, "z", 0, 0, tiled=True).reshape(nz * feats, near * head)
    all_queries = gathered[:, :tokens].reshape(nx * tokens, head)
    all_slots = gathered[:, tokens : tokens + tokens // head].reshape(nx * tokens).astype(jnp.int32)
    frame_ids = jnp.concatenate(
        [held * (h * nx + x) + jnp.arange(held, dtype=jnp.int32) for h in (yh, 1 - yh)]
    )
    mixed = attention(all_queries, keys, values, all_slots, frame_ids, frame_rows)
    back = mixed.reshape(nx, tokens, head)
    attended = lax.dynamic_index_in_dim(back, x, 0, keepdims=False).astype(f32)
    for k in range(1, nx):
        piece = lax.dynamic_index_in_dim(back, (x + k) % nx, 0, keepdims=False)
        attended = attended + shift(piece, "x", k).astype(f32)
    attended, near_weight = tie(attended.astype(bf16), near_weight)
    heads = lax.all_gather(attended, NEAR, axis=1, tiled=True)
    partial = lax.dot_general(
        near_weight, heads, (((1,), (1,)), ((), ())), preferred_element_type=f32
    ).astype(bf16)
    partial, in_left, in_right, down_left, down_right = tie(
        partial, in_left, in_right, down_left, down_right
    )
    half_in, half_down = w_in.shape[1] // 2, w_down.shape[1] // 2
    in_far = shift(in_left[:half_in], "x", 1), shift(in_right[half_in:], "x", -1)
    down_far = shift(down_left[:half_down], "x", 1), shift(down_right[half_down:], "x", -1)
    parts = lax.all_to_all(partial.reshape(nz, feats, tokens), "z", 0, 0, tiled=True)
    projected = jnp.sum(parts.astype(f32), axis=0)
    mid = (hidden_in.T.astype(f32) + jnp.tanh(attn_gate)[:, None] * projected).astype(bf16)
    capacity = 6 * tokens // experts
    selectors, weights = route_tables(expert_ids, gate_fixed, experts, capacity)
    select_rows = (selectors[0] | selectors[1]).astype(bf16)
    sent = lax.dot_general(
        select_rows, mid, (((0,), (1,)), ((), ())), preferred_element_type=f32
    ).astype(bf16)
    sent = jnp.broadcast_to(sent.reshape(1, experts, capacity, feats), (nh, experts, capacity, feats))
    came = lax.all_to_all(sent.reshape(-1, capacity, feats), BOTH, 0, 0, tiled=True)
    rows = came.reshape(nh, experts, capacity, feats).transpose(0, 2, 1, 3)
    (rows,) = tie(rows.reshape(nh * capacity, experts * feats))
    wide = rows.astype(f32)
    mean_square = jnp.mean(wide * wide, axis=1, keepdims=True)
    normed = (wide * lax.rsqrt(mean_square + NORM_EPSILON) * mlp_gain).astype(bf16)
    hidden_units = w_in.shape[3]

    def up(part, weight):
        weight = weight.reshape(weight.shape[0], 2 * hidden_units)
        return jnp.dot(part, weight, preferred_element_type=f32)

    def gated(gate_up):
        return (jax.nn.silu(gate_up[:, :hidden_units]) * gate_up[:, hidden_units:]).astype(bf16)

    ups = [up(normed, weight) for weight in (w_in[0], in_left, in_right)]
    ups.append(up(normed[:, :half_in], in_far[0]) + up(normed[:, half_in:], in_far[1]))
    act = [gated(u) for u in ups]
    weights_down = [w_down[0], down_left, down_right, jnp.concatenate(down_far)]
    down = sum(jnp.dot(p, w, preferred_element_type=f32) for p, w in zip(act, weights_down))
    (down,) = tie(down.astype(bf16))
    dealt = down.reshape(nh, capacity, experts, feats).transpose(0, 2, 1, 3).reshape(-1, capacity, feats)
    back_sums = lax.all_to_all(dealt, BOTH, 0, 0, tiled=True)
    back_sums = back_sums.reshape(nh, experts * capacity, feats).astype(f32)
    came_back = jnp.sum(back_sums, axis=0).astype(bf16)
    mixed_out = sum(
        jnp.dot(s.astype(bf16), came_back, preferred_element_type=f32) * weights[:, k : k + 1]
        for k, s in enumerate(selectors)
    )
    return (mid.T.astype(f32) + mixed_out).astype(bf16)


def solution(mesh):
    fine = Mesh(mesh.devices.reshape(2, 4, 8, 4, 2), SEQ + EXP)
    return jax.shard_map(
        per_device,
        mesh=fine,
        in_specs=(
            P(SEQ, EXP),
            P(SEQ, EXP),
            P(SEQ, None, None),
            P(SEQ, None, None),
            P(SEQ),
            P(),
            P(EXP),
            P(None, EXP),
            P(),
            P(SEQ, None),
            P(SEQ, None),
            P(EXP, None, None, SEQ),
            P(EXP, SEQ, None),
        ),
        out_specs=P(SEQ, EXP),
        check_vma=False,
    )
```

```python
import math

import jax
import jax.numpy as jnp
from jax import lax
from jax.sharding import Mesh
from jax.sharding import PartitionSpec as P

FIXED_SCALE = 1.0 / 65536.0
NORM_EPSILON = 1e-05
MASKED_SCORE = -1e30
SEQ = ("yh", "x")
EXP = ("z", "yl", "core")
NEAR = ("yl", "core")
BOTH = ("yh",) + EXP
f32, bf16 = jnp.float32, jnp.bfloat16


def swap(v, axis):
    return lax.ppermute(v, axis, [(0, 1), (1, 0)])


def shift(v, axis, by):
    n = lax.axis_size(axis)
    return lax.ppermute(v, axis, [(i, (i + by) % n) for i in range(n)])


def tie(*values):
    return lax.optimization_barrier(values)


def spread(v, axis):
    n = lax.axis_size(axis)
    return lax.all_to_all(jnp.broadcast_to(v[None], (n,) + v.shape), axis, 0, 0, tiled=True)


def route_tables(expert_ids, gate_fixed, experts, capacity):
    token_count, top_count = expert_ids.shape
    flat_ids = expert_ids.reshape(-1)
    assigned = flat_ids.shape[0]
    expert_cols = lax.broadcasted_iota(jnp.int32, (assigned, experts), 1)
    matches = flat_ids[:, None] == expert_cols
    before = lax.broadcasted_iota(jnp.int32, (assigned, assigned), 1) < lax.broadcasted_iota(
        jnp.int32, (assigned, assigned), 0
    )
    counts = jnp.dot(before.astype(bf16), matches.astype(bf16), preferred_element_type=f32)
    rank_of = jnp.sum(jnp.where(matches, counts, 0.0), axis=1).astype(jnp.int32)
    slot_of = (flat_ids * capacity + rank_of).reshape(token_count, top_count)
    slot_cols = lax.broadcasted_iota(jnp.int32, (token_count, experts * capacity), 1)
    selectors = [(slot_of[:, k : k + 1] == slot_cols) for k in range(top_count)]
    weights = gate_fixed.astype(f32) * FIXED_SCALE
    return selectors, weights


def attention(queries, keys, values, local_frame, frame_rows):
    width = keys.shape[0]
    scale = 1.0 / math.sqrt(queries.shape[1])
    scores = lax.dot_general(queries, keys, (((1,), (1,)), ((), ())), preferred_element_type=f32) * scale
    column_frame = lax.broadcasted_iota(jnp.int32, (1, width), 1) // frame_rows
    inside = column_frame == local_frame[:, None]
    scores = jnp.where(inside, scores, MASKED_SCORE)
    row_max = jnp.max(scores, axis=1, keepdims=True)
    expon = jnp.exp(scores - row_max)
    row_total = jnp.sum(expon, axis=1, keepdims=True)
    probability = (expon / row_total).astype(bf16)
    mixed = jnp.dot(probability, values, preferred_element_type=f32)
    return jnp.where(local_frame[:, None] >= 0, mixed, 0.0).astype(bf16)


def per_device(
    hidden_in,
    queries,
    frame_keys,
    frame_values,
    cited_frame,
    frame_slot,
    attn_gate,
    out_weight,
    mlp_gain,
    expert_ids,
    gate_fixed,
    w_in,
    w_down,
):
    head = queries.shape[1]
    tokens = queries.shape[0]
    nx, nz, nh = lax.axis_size("x"), lax.axis_size("z"), lax.axis_size("yh")
    experts = lax.axis_size(EXP)
    near = lax.axis_size(NEAR)
    feats = hidden_in.shape[1]
    yh, x, z = lax.axis_index("yh"), lax.axis_index("x"), lax.axis_index("z")
    held, frame_rows = frame_keys.shape[0], frame_keys.shape[1]
    own = jnp.concatenate(
        [
            lax.dynamic_slice_in_dim(frame_keys, z * head, head, 2).reshape(held * frame_rows, head),
            lax.dynamic_slice_in_dim(frame_values, z * head, head, 2).reshape(held * frame_rows, head),
        ],
        axis=0,
    )
    other = swap(own, "yh")
    half = held * frame_rows
    keys = jnp.concatenate([own[:half], other[:half]], axis=0)
    values = jnp.concatenate([own[half:], other[half:]], axis=0)
    frame_cols = lax.broadcasted_iota(jnp.int32, (tokens, frame_slot.shape[0]), 1)
    token_slot = jnp.sum(jnp.where(cited_frame[:, None] == frame_cols, frame_slot[None, :], 0), axis=1)
    slot_rows = jnp.zeros((16, head), bf16).at[: tokens // head].set(
        token_slot.reshape(tokens // head, head).astype(bf16)
    )
    packed = jnp.concatenate([queries, slot_rows])
    gathered = spread(packed, "x")
    half_in, half_down = w_in.shape[1] // 2, w_down.shape[1] // 2
    gathered, turned, down_0, down_1 = tie(
        gathered, out_weight.T, w_down[0, :half_down], w_down[0, half_down:]
    )
    left_down_0, right_down_1 = shift(down_0, "x", 1), shift(down_1, "x", -1)
    turned = turned.reshape(feats, nz, near * head).transpose(1, 0, 2)
    near_weight = lax.all_to_all(turned, "z", 0, 0, tiled=True).reshape(nz * feats, near * head)
    all_queries = gathered[:, :tokens].reshape(nx * tokens, head)
    all_slots = gathered[:, tokens : tokens + tokens // head].reshape(nx * tokens).astype(jnp.int32)
    own_frame = all_slots - held * (yh * nx + x)
    other_frame = all_slots - held * ((1 - yh) * nx + x)
    local_frame = jnp.where(
        (own_frame >= 0) & (own_frame < held),
        own_frame,
        jnp.where((other_frame >= 0) & (other_frame < held), other_frame + held, -1),
    )
    mixed = attention(all_queries, keys, values, local_frame, frame_rows)
    back = mixed.reshape(nx, tokens, head)
    attended = lax.dynamic_index_in_dim(back, x, 0, keepdims=False).astype(f32)
    for k in range(1, nx):
        piece = lax.dynamic_index_in_dim(back, (x + k) % nx, 0, keepdims=False)
        attended = attended + shift(piece, "x", k).astype(f32)
    attended, near_weight, left_down_0, right_down_1 = tie(
        attended.astype(bf16), near_weight, left_down_0, right_down_1
    )
    quarter = half_in // 2
    attended, in_0, in_1, in_q1, in_q2 = tie(
        attended,
        w_in[0, :half_in],
        w_in[0, half_in:],
        w_in[0, quarter:half_in],
        w_in[0, half_in : half_in + quarter],
    )
    left_in_0, right_in_1 = shift(in_0, "x", 1), shift(in_1, "x", -1)
    left_in_q2, right_in_q1 = shift(in_q2, "x", 1), shift(in_q1, "x", -1)
    heads = lax.all_gather(attended, NEAR, axis=1, tiled=True)
    partial = lax.dot_general(
        near_weight, heads, (((1,), (1,)), ((), ())), preferred_element_type=f32
    ).astype(bf16)
    partial, left_in_0, right_in_1 = tie(partial, left_in_0, right_in_1)
    parts = lax.all_to_all(partial.reshape(nz, feats, tokens), "z", 0, 0, tiled=True)
    projected = jnp.sum(parts.astype(f32), axis=0)
    mid = (hidden_in.T.astype(f32) + jnp.tanh(attn_gate)[:, None] * projected).astype(bf16)
    mid, left_in_0, right_in_1, left_in_q2, right_in_q1, down_0, down_1, in_q0, in_q3 = tie(
        mid,
        left_in_0,
        right_in_1,
        left_in_q2,
        right_in_q1,
        down_0,
        down_1,
        w_in[0, :quarter],
        w_in[0, half_in + quarter :],
    )
    left_in_q3, right_in_q0 = shift(in_q3, "x", 1), shift(in_q0, "x", -1)
    far_in_0, far_in_1 = shift(left_in_0, "x", 1), shift(right_in_1, "x", -1)
    left_down_1, right_down_0 = shift(down_1, "x", 1), shift(down_0, "x", -1)
    capacity = 6 * tokens // experts
    selectors, weights = route_tables(expert_ids, gate_fixed, experts, capacity)
    select_rows = (selectors[0] | selectors[1]).astype(bf16)
    sent = lax.dot_general(
        select_rows, mid, (((0,), (1,)), ((), ())), preferred_element_type=f32
    ).astype(bf16)
    sent = jnp.broadcast_to(sent.reshape(1, experts, capacity, feats), (nh, experts, capacity, feats))
    came = lax.all_to_all(sent.reshape(-1, capacity, feats), BOTH, 0, 0, tiled=True)
    rows = came.reshape(nh, experts, capacity, feats).transpose(0, 2, 1, 3)
    rows, left_down_0, right_down_1 = tie(
        rows.reshape(nh * capacity, experts * feats), left_down_0, right_down_1
    )
    far_down_0, far_down_1 = shift(left_down_0, "x", 1), shift(right_down_1, "x", -1)
    wide = rows.astype(f32)
    mean_square = jnp.mean(wide * wide, axis=1, keepdims=True)
    normed = (wide * lax.rsqrt(mean_square + NORM_EPSILON) * mlp_gain).astype(bf16)
    hidden_units = w_in.shape[3]

    def up(part, weight):
        weight = weight.reshape(weight.shape[0], 2 * hidden_units)
        return jnp.dot(part, weight, preferred_element_type=f32)

    def gated(gate_up):
        return (jax.nn.silu(gate_up[:, :hidden_units]) * gate_up[:, hidden_units:]).astype(bf16)

    def up_of(pieces):
        at, total = 0, 0.0
        for piece in pieces:
            total = total + up(normed[:, at : at + piece.shape[0]], piece)
            at += piece.shape[0]
        return total

    ups = [
        up_of(pieces)
        for pieces in (
            (w_in[0],),
            (left_in_0, left_in_q2, left_in_q3),
            (right_in_q0, right_in_q1, right_in_1),
            (far_in_0, far_in_1),
        )
    ]
    act = [gated(u) for u in ups]
    weights_down = [w_down[0]] + [
        jnp.concatenate(pieces)
        for pieces in (
            (left_down_0, left_down_1),
            (right_down_0, right_down_1),
            (far_down_0, far_down_1),
        )
    ]
    down = sum(jnp.dot(p, w, preferred_element_type=f32) for p, w in zip(act, weights_down))
    (down,) = tie(down.astype(bf16))
    dealt = down.reshape(nh, capacity, experts, feats).transpose(0, 2, 1, 3).reshape(-1, capacity, feats)
    back_sums = lax.all_to_all(dealt, BOTH, 0, 0, tiled=True)
    back_sums = back_sums.reshape(nh, experts * capacity, feats).astype(f32)
    came_back = jnp.sum(back_sums, axis=0).astype(bf16)
    mixed_out = sum(
        jnp.dot(s.astype(bf16), came_back, preferred_element_type=f32) * weights[:, k : k + 1]
        for k, s in enumerate(selectors)
    )
    return (mid.T.astype(f32) + mixed_out).astype(bf16)


def solution(mesh):
    fine = Mesh(mesh.devices.reshape(2, 4, 8, 4, 2), SEQ + EXP)
    return jax.shard_map(
        per_device,
        mesh=fine,
        in_specs=(
            P(SEQ, EXP),
            P(SEQ, EXP),
            P(SEQ, None, None),
            P(SEQ, None, None),
            P(SEQ),
            P(),
            P(EXP),
            P(None, EXP),
            P(),
            P(SEQ, None),
            P(SEQ, None),
            P(EXP, None, None, SEQ),
            P(EXP, SEQ, None),
        ),
        out_specs=P(SEQ, EXP),
        check_vma=False,
    )
```

```python
import math

import jax
import jax.numpy as jnp
from jax import lax
from jax.sharding import Mesh
from jax.sharding import PartitionSpec as P

FIXED_SCALE = 1.0 / 65536.0
NORM_EPSILON = 1e-05
MASKED_SCORE = -1e30
SEQ = ("yh", "x")
EXP = ("z", "yl", "core")
NEAR = ("yl", "core")
BOTH = ("yh",) + EXP
f32, bf16 = jnp.float32, jnp.bfloat16


def swap(v, axis):
    return lax.ppermute(v, axis, [(0, 1), (1, 0)])


def shift(v, axis, by):
    n = lax.axis_size(axis)
    return lax.ppermute(v, axis, [(i, (i + by) % n) for i in range(n)])


def tie(*values):
    return lax.optimization_barrier(values)


def route_tables(expert_ids, gate_fixed, experts, capacity):
    token_count, top_count = expert_ids.shape
    flat_ids = expert_ids.reshape(-1)
    assigned = flat_ids.shape[0]
    expert_cols = lax.broadcasted_iota(jnp.int32, (assigned, experts), 1)
    matches = flat_ids[:, None] == expert_cols
    before = lax.broadcasted_iota(jnp.int32, (assigned, assigned), 1) < lax.broadcasted_iota(
        jnp.int32, (assigned, assigned), 0
    )
    counts = jnp.dot(before.astype(bf16), matches.astype(bf16), preferred_element_type=f32)
    rank_of = jnp.sum(jnp.where(matches, counts, 0.0), axis=1).astype(jnp.int32)
    slot_of = (flat_ids * capacity + rank_of).reshape(token_count, top_count)
    slot_cols = lax.broadcasted_iota(jnp.int32, (token_count, experts * capacity), 1)
    selectors = [(slot_of[:, k : k + 1] == slot_cols) for k in range(top_count)]
    weights = gate_fixed.astype(f32) * FIXED_SCALE
    return selectors, weights


def attention(queries, keys, values, local_frame, frame_rows):
    width = keys.shape[0]
    scale = 1.0 / math.sqrt(queries.shape[1])
    scores = lax.dot_general(queries, keys, (((1,), (1,)), ((), ())), preferred_element_type=f32) * scale
    column_frame = lax.broadcasted_iota(jnp.int32, (1, width), 1) // frame_rows
    inside = column_frame == local_frame[:, None]
    scores = jnp.where(inside, scores, MASKED_SCORE)
    row_max = jnp.max(scores, axis=1, keepdims=True)
    expon = jnp.exp(scores - row_max)
    row_total = jnp.sum(expon, axis=1, keepdims=True)
    probability = (expon / row_total).astype(bf16)
    mixed = jnp.dot(probability, values, preferred_element_type=f32)
    return jnp.where(local_frame[:, None] >= 0, mixed, 0.0).astype(bf16)


def per_device(
    hidden_in,
    queries,
    frame_keys,
    frame_values,
    cited_frame,
    frame_slot,
    attn_gate,
    out_weight,
    mlp_gain,
    expert_ids,
    gate_fixed,
    w_in,
    w_down,
):
    head = queries.shape[1]
    tokens = queries.shape[0]
    nx, nz, nh = lax.axis_size("x"), lax.axis_size("z"), lax.axis_size("yh")
    experts = lax.axis_size(EXP)
    near = lax.axis_size(NEAR)
    feats = hidden_in.shape[1]
    yh, x, z = lax.axis_index("yh"), lax.axis_index("x"), lax.axis_index("z")
    held, frame_rows = frame_keys.shape[0], frame_keys.shape[1]
    own = jnp.concatenate(
        [
            lax.dynamic_slice_in_dim(frame_keys, z * head, head, 2).reshape(held * frame_rows, head),
            lax.dynamic_slice_in_dim(frame_values, z * head, head, 2).reshape(held * frame_rows, head),
        ],
        axis=0,
    )
    other = swap(own, "yh")
    half = held * frame_rows
    keys = jnp.concatenate([own[:half], other[:half]], axis=0)
    values = jnp.concatenate([own[half:], other[half:]], axis=0)
    frame_cols = lax.broadcasted_iota(jnp.int32, (tokens, frame_slot.shape[0]), 1)
    token_slot = jnp.sum(jnp.where(cited_frame[:, None] == frame_cols, frame_slot[None, :], 0), axis=1)
    slot_rows = jnp.zeros((16, head), bf16).at[: tokens // head].set(
        token_slot.reshape(tokens // head, head).astype(bf16)
    )
    packed = jnp.concatenate([queries, slot_rows])
    gathered = jnp.stack([packed] + [shift(packed, "x", k) for k in range(1, nx)])
    turned = out_weight.T.reshape(feats, nz, near * head).transpose(1, 0, 2)
    near_weight = lax.all_to_all(turned, "z", 0, 0, tiled=True).reshape(nz * feats, near * head)
    in_rows = jnp.concatenate([w_in[0, :, 0], w_in[0, :, 1]], axis=0)
    in_all = lax.all_gather(in_rows, "x")
    down_all = lax.all_gather(w_down[0], "x", tiled=True)
    all_queries = gathered[:, :tokens].reshape(nx * tokens, head)
    all_slots = gathered[:, tokens : tokens + tokens // head].reshape(nx * tokens).astype(jnp.int32)
    own_frame = all_slots - held * (yh * nx + x)
    other_frame = all_slots - held * ((1 - yh) * nx + x)
    local_frame = jnp.where(
        (own_frame >= 0) & (own_frame < held),
        own_frame,
        jnp.where((other_frame >= 0) & (other_frame < held), other_frame + held, -1),
    )
    mixed = attention(all_queries, keys, values, local_frame, frame_rows)
    back = mixed.reshape(nx, tokens, head)
    attended = sum(
        (shift(back[k], "x", -k) if k else back[k]).astype(f32) for k in range(nx)
    ).astype(bf16)
    heads = lax.all_gather(attended, NEAR, axis=1, tiled=True)
    partial = lax.dot_general(
        near_weight, heads, (((1,), (1,)), ((), ())), preferred_element_type=f32
    ).astype(bf16)
    parts = lax.all_to_all(partial.reshape(nz, feats, tokens), "z", 0, 0, tiled=True)
    projected = jnp.sum(parts.astype(f32), axis=0)
    mid = (hidden_in.T.astype(f32) + jnp.tanh(attn_gate)[:, None] * projected).astype(bf16)
    capacity = 6 * tokens // experts
    selectors, weights = route_tables(expert_ids, gate_fixed, experts, capacity)
    select_rows = (selectors[0] | selectors[1]).astype(bf16)
    sent = lax.dot_general(
        select_rows, mid, (((0,), (1,)), ((), ())), preferred_element_type=f32
    ).astype(bf16)
    sent = jnp.broadcast_to(sent.reshape(1, experts, capacity, feats), (nh, experts, capacity, feats))
    came = lax.all_to_all(sent.reshape(-1, capacity, feats), BOTH, 0, 0, tiled=True)
    rows = came.reshape(nh, experts, capacity, feats).transpose(0, 2, 1, 3)
    (rows,) = tie(rows.reshape(nh * capacity, experts * feats))
    wide = rows.astype(f32)
    mean_square = jnp.mean(wide * wide, axis=1, keepdims=True)
    normed = (wide * lax.rsqrt(mean_square + NORM_EPSILON) * mlp_gain).astype(bf16)
    width = w_in.shape[1]

    def gated(weight):
        gate = jnp.dot(normed, weight[:width], preferred_element_type=f32)
        up = jnp.dot(normed, weight[width:], preferred_element_type=f32)
        return (jax.nn.silu(gate) * up).astype(bf16)

    act = jnp.concatenate([gated(in_all[k]) for k in range(nx)], axis=1)
    down = jnp.dot(act, down_all, preferred_element_type=f32)
    (down,) = tie(down.astype(bf16))
    dealt = down.reshape(nh, capacity, experts, feats).transpose(0, 2, 1, 3).reshape(-1, capacity, feats)
    back_sums = lax.all_to_all(dealt, BOTH, 0, 0, tiled=True)
    back_sums = back_sums.reshape(nh, experts * capacity, feats).astype(f32)
    came_back = jnp.sum(back_sums, axis=0).astype(bf16)
    mixed_out = sum(
        jnp.dot(s.astype(bf16), came_back, preferred_element_type=f32) * weights[:, k : k + 1]
        for k, s in enumerate(selectors)
    )
    return (mid.T.astype(f32) + mixed_out).astype(bf16)


def solution(mesh):
    fine = Mesh(mesh.devices.reshape(2, 4, 8, 4, 2), SEQ + EXP)
    return jax.shard_map(
        per_device,
        mesh=fine,
        in_specs=(
            P(SEQ, EXP),
            P(SEQ, EXP),
            P(SEQ, None, None),
            P(SEQ, None, None),
            P(SEQ),
            P(),
            P(EXP),
            P(None, EXP),
            P(),
            P(SEQ, None),
            P(SEQ, None),
            P(EXP, None, None, SEQ),
            P(EXP, SEQ, None),
        ),
        out_specs=P(SEQ, EXP),
        check_vma=False,
    )
```

```python
import functools
import math

import jax
import jax.numpy as jnp
import numpy as np
from jax import lax
from jax.experimental import pallas as pl
from jax.experimental.pallas import tpu as pltpu
from jax.sharding import Mesh
from jax.sharding import PartitionSpec as P

FIXED_SCALE = 1.0 / 65536.0
NORM_EPSILON = 1e-05
MASKED_SCORE = -1e30
SEQ = ("yh", "x")
EXP = ("z", "yl", "core")
NEAR = ("yl", "core")
BOTH = ("yh",) + EXP
f32, bf16 = jnp.float32, jnp.bfloat16


def swap(v, axis):
    return lax.ppermute(v, axis, [(0, 1), (1, 0)])


def shift(v, axis, by):
    n = lax.axis_size(axis)
    return lax.ppermute(v, axis, [(i, (i + by) % n) for i in range(n)])


def tie(*values):
    return lax.optimization_barrier(values)


def slots_of(expert_ids, capacity, experts):
    token_count, top_count = expert_ids.shape
    flat_ids = expert_ids.reshape(-1)
    assigned = flat_ids.shape[0]
    expert_cols = lax.broadcasted_iota(jnp.int32, (assigned, experts), 1)
    matches = flat_ids[:, None] == expert_cols
    before = lax.broadcasted_iota(jnp.int32, (assigned, assigned), 1) < lax.broadcasted_iota(
        jnp.int32, (assigned, assigned), 0
    )
    counts = jnp.dot(before.astype(bf16), matches.astype(bf16), preferred_element_type=f32)
    rank_of = jnp.sum(jnp.where(matches, counts, 0.0), axis=1).astype(jnp.int32)
    return (flat_ids * capacity + rank_of).reshape(token_count, top_count).T


def row_slots(experts, capacity, padded):
    half = capacity // 2
    row = np.arange(experts * padded)
    at = row % padded
    return np.where(at < half, row // padded * capacity + at, -4 * capacity).astype(np.int32)[:, None]


def chosen(rows, slot):
    return jnp.where(rows == slot, 1.0, 0.0)


def dispatch_kernel(experts, half, padded, parts, hidden, gate, slots, rows, mid_out, sent):
    summed = jnp.sum(parts[...].astype(f32), axis=0)
    mid = (hidden[...].astype(f32) + jnp.tanh(gate[...]) * summed).astype(bf16)
    mid_out[...] = mid
    nothing = jnp.zeros_like(mid)
    low = rows[...]
    first, second = slots[0:1], slots[1:2]
    total = 0.0
    for at, wide in ((low, (mid, nothing)), (low + half, (nothing, mid))):
        pick = (chosen(at, first) + chosen(at, second)).astype(bf16)
        total = total + lax.dot_general(
            pick, jnp.concatenate(wide, axis=0), (((1,), (1,)), ((), ())), preferred_element_type=f32
        )
    for e in range(experts):
        block = total[e * padded : e * padded + half].astype(bf16)
        for copy in range(sent.shape[0] // experts):
            sent[copy * experts + e] = block


def assemble_kernel(experts, half, padded, came, gain, normed, wide):
    wide[...] = jnp.zeros_like(wide)
    lanes = came.shape[2]
    left = lax.broadcasted_iota(jnp.int32, (half, lanes), 1) < lanes // 2
    for group in range(came.shape[0] // experts):
        for pair in range(experts // 2):
            one = came[group * experts + 2 * pair].astype(f32)
            two = came[group * experts + 2 * pair + 1].astype(f32)
            cols = pl.ds(pair * lanes, lanes)
            at = 2 * group * padded
            wide[pl.ds(at, half), cols] = jnp.where(left, one, pltpu.roll(two, lanes // 2, 1))
            wide[pl.ds(at + padded, half), cols] = jnp.where(left, pltpu.roll(one, lanes // 2, 1), two)
    rows = wide[...]
    mean_square = jnp.mean(rows * rows, axis=1, keepdims=True)
    normed[...] = (rows * lax.rsqrt(mean_square + NORM_EPSILON) * gain[...]).astype(bf16)


def expert_kernel(experts, half, padded, place, normed, weights, *rest):
    del place
    *downs, out, wide = rest
    step = pl.program_id(0)
    inner = normed.shape[1]
    gate = jnp.dot(normed[...], weights[0, :inner], preferred_element_type=f32)
    up = jnp.dot(normed[...], weights[0, inner:], preferred_element_type=f32)
    act = (gate / (1.0 + jnp.exp(-gate)) * up).astype(bf16)
    for k, down in enumerate(downs):

        @pl.when(step == k)
        def _():
            product = jnp.dot(act, down[...], preferred_element_type=f32)
            wide[...] = product if k == 0 else wide[...] + product

    @pl.when(step == len(downs) - 1)
    def _():
        lanes = out.shape[2]
        left = lax.broadcasted_iota(jnp.int32, (half, lanes), 1) < lanes // 2
        for group in range(out.shape[0] // experts):
            for pair in range(experts // 2):
                cols = pl.ds(pair * lanes, lanes)
                at = 2 * group * padded
                low = wide[pl.ds(at, half), cols]
                high = wide[pl.ds(at + padded, half), cols]
                out[group * experts + 2 * pair] = jnp.where(
                    left, low, pltpu.roll(high, lanes // 2, 1)
                ).astype(bf16)
                out[group * experts + 2 * pair + 1] = jnp.where(
                    left, pltpu.roll(low, lanes // 2, 1), high
                ).astype(bf16)


def combine_kernel(experts, half, padded, back, mid, slots, fixed, rows, out, table):
    table[...] = jnp.zeros_like(table)
    for e in range(experts):
        total = back[e].astype(f32)
        for copy in range(1, back.shape[0] // experts):
            total = total + back[copy * experts + e].astype(f32)
        table[pl.ds(e * padded, half), :] = total
    rounded = table[...].astype(bf16)
    feats = mid.shape[0]
    low = rows[...]
    total = mid[...].astype(f32)
    for k in range(slots.shape[0]):
        slot = slots[k : k + 1]
        picked = 0.0
        for at, begin in ((low, 0), (low + half, feats)):
            both = lax.dot_general(
                rounded, chosen(at, slot).astype(bf16), (((0,), (0,)), ((), ())), preferred_element_type=f32
            )
            picked = picked + both[begin : begin + feats]
        total = total + picked * (fixed[k : k + 1].astype(f32) * FIXED_SCALE)
    out[...] = total.astype(bf16)


def local_kernel(body, *out_shapes, scratch=()):
    return pl.pallas_call(
        body,
        out_shape=out_shapes,
        scratch_shapes=scratch,
        compiler_params=pltpu.CompilerParams(vmem_limit_bytes=40 * 1024 * 1024),
    )


def attention(queries, keys, values, local_frame, frame_rows):
    width = keys.shape[0]
    scale = 1.0 / math.sqrt(queries.shape[1])
    scores = lax.dot_general(queries, keys, (((1,), (1,)), ((), ())), preferred_element_type=f32) * scale
    column_frame = lax.broadcasted_iota(jnp.int32, (1, width), 1) // frame_rows
    inside = column_frame == local_frame[:, None]
    scores = jnp.where(inside, scores, MASKED_SCORE)
    row_max = jnp.max(scores, axis=1, keepdims=True)
    expon = jnp.exp(scores - row_max)
    row_total = jnp.sum(expon, axis=1, keepdims=True)
    probability = (expon / row_total).astype(bf16)
    mixed = jnp.dot(probability, values, preferred_element_type=f32)
    return jnp.where(local_frame[:, None] >= 0, mixed, 0.0).astype(bf16)


def per_device(
    hidden_in,
    queries,
    frame_keys,
    frame_values,
    cited_frame,
    frame_slot,
    attn_gate,
    out_weight,
    mlp_gain,
    expert_ids,
    gate_fixed,
    w_in,
    w_down,
):
    head = queries.shape[1]
    tokens = queries.shape[0]
    nx, nz, nh = lax.axis_size("x"), lax.axis_size("z"), lax.axis_size("yh")
    experts = lax.axis_size(EXP)
    near = lax.axis_size(NEAR)
    feats = hidden_in.shape[1]
    yh, x, z = lax.axis_index("yh"), lax.axis_index("x"), lax.axis_index("z")
    held, frame_rows = frame_keys.shape[0], frame_keys.shape[1]
    own = jnp.concatenate(
        [
            lax.dynamic_slice_in_dim(frame_keys, z * head, head, 2).reshape(held * frame_rows, head),
            lax.dynamic_slice_in_dim(frame_values, z * head, head, 2).reshape(held * frame_rows, head),
        ],
        axis=0,
    )
    other = swap(own, "yh")
    half = held * frame_rows
    keys = jnp.concatenate([own[:half], other[:half]], axis=0)
    values = jnp.concatenate([own[half:], other[half:]], axis=0)
    frame_cols = lax.broadcasted_iota(jnp.int32, (tokens, frame_slot.shape[0]), 1)
    token_slot = jnp.sum(jnp.where(cited_frame[:, None] == frame_cols, frame_slot[None, :], 0), axis=1)
    slot_rows = jnp.zeros((16, head), bf16).at[: tokens // head].set(
        token_slot.reshape(tokens // head, head).astype(bf16)
    )
    packed = jnp.concatenate([queries, slot_rows])
    gathered = jnp.stack([packed] + [shift(packed, "x", k) for k in range(1, nx)])
    gathered, wide_in = tie(gathered, w_in[0])
    in_all = lax.all_gather(jnp.concatenate([wide_in[:, 0], wide_in[:, 1]], axis=0), "x")
    turned = out_weight.T.reshape(feats, nz, near * head).transpose(1, 0, 2)
    near_weight = lax.all_to_all(turned, "z", 0, 0, tiled=True).reshape(nz * feats, near * head)
    all_queries = gathered[:, :tokens].reshape(nx * tokens, head)
    all_slots = gathered[:, tokens : tokens + tokens // head].reshape(nx * tokens).astype(jnp.int32)
    own_frame = all_slots - held * (yh * nx + x)
    other_frame = all_slots - held * ((1 - yh) * nx + x)
    local_frame = jnp.where(
        (own_frame >= 0) & (own_frame < held),
        own_frame,
        jnp.where((other_frame >= 0) & (other_frame < held), other_frame + held, -1),
    )
    mixed = attention(all_queries, keys, values, local_frame, frame_rows)
    back = mixed.reshape(nx, tokens, head)
    attended = sum(
        (shift(back[k], "x", -k) if k else back[k]).astype(f32) for k in range(nx)
    ).astype(bf16)
    attended, own_down = tie(attended, w_down[0])
    down_pieces = [own_down] + [shift(own_down, "x", k) for k in range(1, nx)]
    heads = lax.all_gather(attended, NEAR, axis=1, tiled=True)
    partial = lax.dot_general(
        near_weight, heads, (((1,), (1,)), ((), ())), preferred_element_type=f32
    ).astype(bf16)
    parts = lax.all_to_all(partial.reshape(nz, feats, tokens), "z", 0, 0, tiled=True)
    capacity = 6 * tokens // experts
    half, padded = capacity // 2, -(-(capacity // 2) // 8) * 8
    lanes = 2 * feats
    table = row_slots(experts, capacity, padded)
    slots = slots_of(expert_ids, capacity, experts)
    mid, sent = local_kernel(
        functools.partial(dispatch_kernel, experts, half, padded),
        jax.ShapeDtypeStruct((feats, tokens), bf16),
        jax.ShapeDtypeStruct((nh * experts, half, lanes), bf16),
    )(parts, hidden_in.T, attn_gate[:, None], slots, table)
    sent, down_pieces[1], down_pieces[3] = tie(sent, down_pieces[1], down_pieces[3])
    came = lax.all_to_all(sent, BOTH, 0, 0, tiled=True)
    came, *down_pieces = tie(came, *down_pieces)
    rows = 2 * nh * padded
    (normed,) = local_kernel(
        functools.partial(assemble_kernel, experts, half, padded),
        jax.ShapeDtypeStruct((rows, experts * feats), bf16),
        scratch=(pltpu.VMEM((rows, experts * feats), f32),),
    )(came, mlp_gain[None])

    whole = lambda v: pl.BlockSpec(v.shape, lambda k, place: (0,) * v.ndim)
    dealt = pl.pallas_call(
        functools.partial(expert_kernel, experts, half, padded),
        grid_spec=pltpu.PrefetchScalarGridSpec(
            num_scalar_prefetch=1,
            grid=(nx,),
            in_specs=[
                whole(normed),
                pl.BlockSpec((1,) + in_all.shape[1:], lambda k, place: ((place[0] + nx - k) % nx, 0, 0)),
            ]
            + [whole(piece) for piece in down_pieces],
            out_specs=whole(came),
            scratch_shapes=[pltpu.VMEM((rows, experts * feats), f32)],
        ),
        out_shape=jax.ShapeDtypeStruct(came.shape, bf16),
        compiler_params=pltpu.CompilerParams(vmem_limit_bytes=40 * 1024 * 1024),
    )(x[None], normed, in_all, *down_pieces)
    back_sums = lax.all_to_all(dealt, BOTH, 0, 0, tiled=True)
    (out,) = local_kernel(
        functools.partial(combine_kernel, experts, half, padded),
        jax.ShapeDtypeStruct((feats, tokens), bf16),
        scratch=(pltpu.VMEM((experts * padded, lanes), f32),),
    )(back_sums, mid, slots, gate_fixed.T, table)
    return out.T


def solution(mesh):
    fine = Mesh(mesh.devices.reshape(2, 4, 8, 4, 2), SEQ + EXP)
    return jax.shard_map(
        per_device,
        mesh=fine,
        in_specs=(
            P(SEQ, EXP),
            P(SEQ, EXP),
            P(SEQ, None, None),
            P(SEQ, None, None),
            P(SEQ),
            P(),
            P(EXP),
            P(None, EXP),
            P(),
            P(SEQ, None),
            P(SEQ, None),
            P(EXP, None, None, SEQ),
            P(EXP, SEQ, None),
        ),
        out_specs=P(SEQ, EXP),
        check_vma=False,
    )
```

```python
import functools
import math

import jax
import jax.numpy as jnp
import numpy as np
from jax import lax
from jax.experimental import pallas as pl
from jax.experimental.pallas import tpu as pltpu
from jax.sharding import Mesh
from jax.sharding import PartitionSpec as P

FIXED_SCALE = 1.0 / 65536.0
NORM_EPSILON = 1e-05
MASKED_SCORE = -1e30
SEQ = ("yh", "x")
EXP = ("z", "yl", "core")
NEAR = ("yl", "core")
BOTH = ("yh",) + EXP
f32, bf16 = jnp.float32, jnp.bfloat16


def swap(v, axis):
    return lax.ppermute(v, axis, [(0, 1), (1, 0)])


def shift(v, axis, by):
    n = lax.axis_size(axis)
    return lax.ppermute(v, axis, [(i, (i + by) % n) for i in range(n)])


def tie(*values):
    return lax.optimization_barrier(values)


def slots_of(expert_ids, capacity, experts):
    token_count, top_count = expert_ids.shape
    flat_ids = expert_ids.reshape(-1)
    assigned = flat_ids.shape[0]
    expert_cols = lax.broadcasted_iota(jnp.int32, (assigned, experts), 1)
    matches = flat_ids[:, None] == expert_cols
    before = lax.broadcasted_iota(jnp.int32, (assigned, assigned), 1) < lax.broadcasted_iota(
        jnp.int32, (assigned, assigned), 0
    )
    counts = jnp.dot(before.astype(bf16), matches.astype(bf16), preferred_element_type=f32)
    rank_of = jnp.sum(jnp.where(matches, counts, 0.0), axis=1).astype(jnp.int32)
    return (flat_ids * capacity + rank_of).reshape(token_count, top_count).T


def row_slots(experts, capacity, padded):
    half = capacity // 2
    row = np.arange(experts * padded)
    at = row % padded
    return np.where(at < half, row // padded * capacity + at, -4 * capacity).astype(np.int32)[:, None]


def chosen(rows, slot):
    return jnp.where(rows == slot, 1.0, 0.0)


def dispatch_kernel(experts, half, padded, parts, hidden, gate, slots, rows, mid_out, sent):
    summed = jnp.sum(parts[...].astype(f32), axis=0)
    mid = (hidden[...].astype(f32) + jnp.tanh(gate[...]) * summed).astype(bf16)
    mid_out[...] = mid
    nothing = jnp.zeros_like(mid)
    low = rows[...]
    first, second = slots[0:1], slots[1:2]
    total = 0.0
    for at, wide in ((low, (mid, nothing)), (low + half, (nothing, mid))):
        pick = (chosen(at, first) + chosen(at, second)).astype(bf16)
        total = total + lax.dot_general(
            pick, jnp.concatenate(wide, axis=0), (((1,), (1,)), ((), ())), preferred_element_type=f32
        )
    for e in range(experts):
        block = total[e * padded : e * padded + half].astype(bf16)
        for copy in range(sent.shape[0] // experts):
            sent[copy * experts + e] = block


def assemble_kernel(experts, half, padded, came, gain, normed, wide):
    wide[...] = jnp.zeros_like(wide)
    lanes = came.shape[2]
    left = lax.broadcasted_iota(jnp.int32, (half, lanes), 1) < lanes // 2
    for group in range(came.shape[0] // experts):
        for pair in range(experts // 2):
            one = came[group * experts + 2 * pair].astype(f32)
            two = came[group * experts + 2 * pair + 1].astype(f32)
            cols = pl.ds(pair * lanes, lanes)
            at = 2 * group * padded
            wide[pl.ds(at, half), cols] = jnp.where(left, one, pltpu.roll(two, lanes // 2, 1))
            wide[pl.ds(at + padded, half), cols] = jnp.where(left, pltpu.roll(one, lanes // 2, 1), two)
    rows = wide[...]
    mean_square = jnp.mean(rows * rows, axis=1, keepdims=True)
    normed[...] = (rows * lax.rsqrt(mean_square + NORM_EPSILON) * gain[...]).astype(bf16)


def expert_kernel(experts, half, padded, place, normed, own, left_in, right_in, far_gate, far_up, downs, out, wide):
    nx = downs.shape[0]
    inner = normed.shape[1]
    rows = normed[...]
    for k, (gates, ups) in enumerate(
        (
            (own.at[:inner], own.at[inner:]),
            (left_in.at[:inner], left_in.at[inner:]),
            (right_in.at[:inner], right_in.at[inner:]),
            (far_gate, far_up),
        )
    ):
        gate = jnp.dot(rows, gates[...], preferred_element_type=f32)
        up = jnp.dot(rows, ups[...], preferred_element_type=f32)
        act = (gate / (1.0 + jnp.exp(-gate)) * up).astype(bf16)
        origin = (place[0] + (0, nx - 1, 1, 2)[k]) % nx
        product = jnp.dot(act, downs[origin], preferred_element_type=f32)
        wide[...] = product if k == 0 else wide[...] + product
    lanes = out.shape[2]
    left = lax.broadcasted_iota(jnp.int32, (half, lanes), 1) < lanes // 2
    for group in range(out.shape[0] // experts):
        for pair in range(experts // 2):
            cols = pl.ds(pair * lanes, lanes)
            at = 2 * group * padded
            low = wide[pl.ds(at, half), cols]
            high = wide[pl.ds(at + padded, half), cols]
            out[group * experts + 2 * pair] = jnp.where(left, low, pltpu.roll(high, lanes // 2, 1)).astype(bf16)
            out[group * experts + 2 * pair + 1] = jnp.where(
                left, pltpu.roll(low, lanes // 2, 1), high
            ).astype(bf16)


def combine_kernel(experts, half, padded, back, mid, slots, fixed, rows, out, table):
    table[...] = jnp.zeros_like(table)
    for e in range(experts):
        total = back[e].astype(f32)
        for copy in range(1, back.shape[0] // experts):
            total = total + back[copy * experts + e].astype(f32)
        table[pl.ds(e * padded, half), :] = total
    rounded = table[...].astype(bf16)
    feats = mid.shape[0]
    low = rows[...]
    total = mid[...].astype(f32)
    for k in range(slots.shape[0]):
        slot = slots[k : k + 1]
        picked = 0.0
        for at, begin in ((low, 0), (low + half, feats)):
            both = lax.dot_general(
                rounded, chosen(at, slot).astype(bf16), (((0,), (0,)), ((), ())), preferred_element_type=f32
            )
            picked = picked + both[begin : begin + feats]
        total = total + picked * (fixed[k : k + 1].astype(f32) * FIXED_SCALE)
    out[...] = total.astype(bf16)


def local_kernel(body, *out_shapes, scratch=()):
    return pl.pallas_call(
        body,
        out_shape=out_shapes,
        scratch_shapes=scratch,
        compiler_params=pltpu.CompilerParams(vmem_limit_bytes=40 * 1024 * 1024),
    )


def attention(queries, keys, values, local_frame, frame_rows):
    width = keys.shape[0]
    scale = 1.0 / math.sqrt(queries.shape[1])
    scores = lax.dot_general(queries, keys, (((1,), (1,)), ((), ())), preferred_element_type=f32) * scale
    column_frame = lax.broadcasted_iota(jnp.int32, (1, width), 1) // frame_rows
    inside = column_frame == local_frame[:, None]
    scores = jnp.where(inside, scores, MASKED_SCORE)
    row_max = jnp.max(scores, axis=1, keepdims=True)
    expon = jnp.exp(scores - row_max)
    row_total = jnp.sum(expon, axis=1, keepdims=True)
    probability = (expon / row_total).astype(bf16)
    mixed = jnp.dot(probability, values, preferred_element_type=f32)
    return jnp.where(local_frame[:, None] >= 0, mixed, 0.0).astype(bf16)


def per_device(
    hidden_in,
    queries,
    frame_keys,
    frame_values,
    cited_frame,
    frame_slot,
    attn_gate,
    out_weight,
    mlp_gain,
    expert_ids,
    gate_fixed,
    w_in,
    w_down,
):
    head = queries.shape[1]
    tokens = queries.shape[0]
    nx, nz, nh = lax.axis_size("x"), lax.axis_size("z"), lax.axis_size("yh")
    experts = lax.axis_size(EXP)
    near = lax.axis_size(NEAR)
    feats = hidden_in.shape[1]
    yh, x, z = lax.axis_index("yh"), lax.axis_index("x"), lax.axis_index("z")
    held, frame_rows = frame_keys.shape[0], frame_keys.shape[1]
    own = jnp.concatenate(
        [
            lax.dynamic_slice_in_dim(frame_keys, z * head, head, 2).reshape(held * frame_rows, head),
            lax.dynamic_slice_in_dim(frame_values, z * head, head, 2).reshape(held * frame_rows, head),
        ],
        axis=0,
    )
    frame_cols = lax.broadcasted_iota(jnp.int32, (tokens, frame_slot.shape[0]), 1)
    token_slot = jnp.sum(jnp.where(cited_frame[:, None] == frame_cols, frame_slot[None, :], 0), axis=1)
    slot_rows = jnp.zeros((16, head), bf16).at[: tokens // head].set(
        token_slot.reshape(tokens // head, head).astype(bf16)
    )
    packed, own = tie(jnp.concatenate([queries, slot_rows]), own)
    other = swap(own, "yh")
    gathered = jnp.stack([packed] + [shift(packed, "x", k) for k in range(1, nx)])
    down_all = lax.all_gather(w_down[0], "x")
    gathered, wide_in = tie(gathered, w_in[0])
    own_in = jnp.concatenate([wide_in[:, 0], wide_in[:, 1]], axis=0)
    turned = out_weight.T.reshape(feats, nz, near * head).transpose(1, 0, 2)
    near_weight = lax.all_to_all(turned, "z", 0, 0, tiled=True).reshape(nz * feats, near * head)
    all_queries = gathered[:, :tokens].reshape(nx * tokens, head)
    all_slots = gathered[:, tokens : tokens + tokens // head].reshape(nx * tokens).astype(jnp.int32)
    own_frame = all_slots - held * (yh * nx + x)
    other_frame = all_slots - held * ((1 - yh) * nx + x)
    local_frame = jnp.where(
        (own_frame >= 0) & (own_frame < held),
        own_frame,
        jnp.where((other_frame >= 0) & (other_frame < held), other_frame + held, -1),
    )
    half = held * frame_rows
    keys = jnp.concatenate([own[:half], other[:half]], axis=0)
    values = jnp.concatenate([own[half:], other[half:]], axis=0)
    mixed = attention(all_queries, keys, values, local_frame, frame_rows)
    back = mixed.reshape(nx, tokens, head)
    attended = sum(
        (shift(back[k], "x", -k) if k else back[k]).astype(f32) for k in range(nx)
    ).astype(bf16)
    attended, own_in = tie(attended, own_in)
    left_in, right_in = shift(own_in, "x", 1), shift(own_in, "x", -1)
    heads = lax.all_gather(attended, NEAR, axis=1, tiled=True)
    partial = lax.dot_general(
        near_weight, heads, (((1,), (1,)), ((), ())), preferred_element_type=f32
    ).astype(bf16)
    parts = lax.all_to_all(partial.reshape(nz, feats, tokens), "z", 0, 0, tiled=True)
    capacity = 6 * tokens // experts
    half, padded = capacity // 2, -(-(capacity // 2) // 8) * 8
    lanes = 2 * feats
    table = row_slots(experts, capacity, padded)
    slots = slots_of(expert_ids, capacity, experts)
    mid, sent = local_kernel(
        functools.partial(dispatch_kernel, experts, half, padded),
        jax.ShapeDtypeStruct((feats, tokens), bf16),
        jax.ShapeDtypeStruct((nh * experts, half, lanes), bf16),
    )(parts, hidden_in.T, attn_gate[:, None], slots, table)
    sent, left_in, right_in = tie(sent, left_in, right_in)
    width = w_in.shape[1]
    far_gate, far_up = shift(left_in[:width], "x", 1), shift(right_in[width:], "x", -1)
    came = lax.all_to_all(sent, BOTH, 0, 0, tiled=True)
    rows = 2 * nh * padded
    (normed,) = local_kernel(
        functools.partial(assemble_kernel, experts, half, padded),
        jax.ShapeDtypeStruct((rows, experts * feats), bf16),
        scratch=(pltpu.VMEM((rows, experts * feats), f32),),
    )(came, mlp_gain[None])

    in_vmem = pl.BlockSpec(memory_space=pltpu.VMEM)
    dealt = pl.pallas_call(
        functools.partial(expert_kernel, experts, half, padded),
        in_specs=[pl.BlockSpec(memory_space=pltpu.SMEM)] + [in_vmem] * 7,
        out_specs=in_vmem,
        out_shape=jax.ShapeDtypeStruct(came.shape, bf16),
        scratch_shapes=[pltpu.VMEM((rows, experts * feats), f32)],
        compiler_params=pltpu.CompilerParams(vmem_limit_bytes=40 * 1024 * 1024),
    )(x[None], normed, own_in, left_in, right_in, far_gate, far_up, down_all)
    back_sums = lax.all_to_all(dealt, BOTH, 0, 0, tiled=True)
    (out,) = local_kernel(
        functools.partial(combine_kernel, experts, half, padded),
        jax.ShapeDtypeStruct((feats, tokens), bf16),
        scratch=(pltpu.VMEM((experts * padded, lanes), f32),),
    )(back_sums, mid, slots, gate_fixed.T, table)
    return out.T


def solution(mesh):
    fine = Mesh(mesh.devices.reshape(2, 4, 8, 4, 2), SEQ + EXP)
    return jax.shard_map(
        per_device,
        mesh=fine,
        in_specs=(
            P(SEQ, EXP),
            P(SEQ, EXP),
            P(SEQ, None, None),
            P(SEQ, None, None),
            P(SEQ),
            P(),
            P(EXP),
            P(None, EXP),
            P(),
            P(SEQ, None),
            P(SEQ, None),
            P(EXP, None, None, SEQ),
            P(EXP, SEQ, None),
        ),
        out_specs=P(SEQ, EXP),
        check_vma=False,
    )
```

```python
import functools
import math

import jax
import jax.numpy as jnp
import numpy as np
from jax import lax
from jax.experimental import pallas as pl
from jax.experimental.pallas import tpu as pltpu
from jax.sharding import Mesh
from jax.sharding import PartitionSpec as P

FIXED_SCALE = 1.0 / 65536.0
NORM_EPSILON = 1e-05
MASKED_SCORE = -1e30
SEQ = ("yh", "x")
EXP = ("z", "yl", "core")
NEAR = ("yl", "core")
BOTH = ("yh",) + EXP
f32, bf16 = jnp.float32, jnp.bfloat16


def swap(v, axis):
    return lax.ppermute(v, axis, [(0, 1), (1, 0)])


def shift(v, axis, by):
    n = lax.axis_size(axis)
    return lax.ppermute(v, axis, [(i, (i + by) % n) for i in range(n)])


def tie(*values):
    return lax.optimization_barrier(values)


def spread(v, axis):
    n = lax.axis_size(axis)
    return lax.all_to_all(jnp.broadcast_to(v[None], (n,) + v.shape), axis, 0, 0, tiled=True)


def slots_of(expert_ids, capacity, experts):
    token_count, top_count = expert_ids.shape
    flat_ids = expert_ids.reshape(-1)
    assigned = flat_ids.shape[0]
    expert_cols = lax.broadcasted_iota(jnp.int32, (assigned, experts), 1)
    matches = flat_ids[:, None] == expert_cols
    before = lax.broadcasted_iota(jnp.int32, (assigned, assigned), 1) < lax.broadcasted_iota(
        jnp.int32, (assigned, assigned), 0
    )
    counts = jnp.dot(before.astype(bf16), matches.astype(bf16), preferred_element_type=f32)
    rank_of = jnp.sum(jnp.where(matches, counts, 0.0), axis=1).astype(jnp.int32)
    return (flat_ids * capacity + rank_of).reshape(token_count, top_count).T


def row_slots(experts, capacity, padded):
    half = capacity // 2
    row = np.arange(experts * padded)
    at = row % padded
    return np.where(at < half, row // padded * capacity + at, -4 * capacity).astype(np.int32)[:, None]


def chosen(rows, slot):
    return jnp.where(rows == slot, 1.0, 0.0)


def dispatch_kernel(experts, half, padded, parts, hidden, gate, slots, rows, mid_out, sent):
    summed = jnp.sum(parts[...].astype(f32), axis=0)
    mid = (hidden[...].astype(f32) + jnp.tanh(gate[...]) * summed).astype(bf16)
    mid_out[...] = mid
    nothing = jnp.zeros_like(mid)
    low = rows[...]
    first, second = slots[0:1], slots[1:2]
    total = 0.0
    for at, wide in ((low, (mid, nothing)), (low + half, (nothing, mid))):
        pick = (chosen(at, first) + chosen(at, second)).astype(bf16)
        total = total + lax.dot_general(
            pick, jnp.concatenate(wide, axis=0), (((1,), (1,)), ((), ())), preferred_element_type=f32
        )
    for e in range(experts):
        block = total[e * padded : e * padded + half].astype(bf16)
        for copy in range(sent.shape[0] // experts):
            sent[copy * experts + e] = block


def assemble_kernel(experts, half, padded, came, gain, normed, wide):
    wide[...] = jnp.zeros_like(wide)
    lanes = came.shape[2]
    left = lax.broadcasted_iota(jnp.int32, (half, lanes), 1) < lanes // 2
    for group in range(came.shape[0] // experts):
        for pair in range(experts // 2):
            one = came[group * experts + 2 * pair].astype(f32)
            two = came[group * experts + 2 * pair + 1].astype(f32)
            cols = pl.ds(pair * lanes, lanes)
            at = 2 * group * padded
            wide[pl.ds(at, half), cols] = jnp.where(left, one, pltpu.roll(two, lanes // 2, 1))
            wide[pl.ds(at + padded, half), cols] = jnp.where(left, pltpu.roll(one, lanes // 2, 1), two)
    rows = wide[...]
    mean_square = jnp.mean(rows * rows, axis=1, keepdims=True)
    normed[...] = (rows * lax.rsqrt(mean_square + NORM_EPSILON) * gain[...]).astype(bf16)


def expert_kernel(
    experts, half, padded, place, normed, gates, own_up, left_up, right_up, far_low, far_high, downs, out, wide
):
    nx = downs.shape[0]
    rows = normed[...]
    cut = far_low.shape[0]
    for k, ups in enumerate(((own_up,), (left_up,), (right_up,), (far_low, far_high))):
        origin = (place[0] + (0, nx - 1, 1, 2)[k]) % nx
        gate = jnp.dot(rows, gates[origin], preferred_element_type=f32)
        if len(ups) == 1:
            up = jnp.dot(rows, ups[0][...], preferred_element_type=f32)
        else:
            up = jnp.dot(rows[:, :cut], ups[0][...], preferred_element_type=f32)
            up = up + jnp.dot(rows[:, cut:], ups[1][...], preferred_element_type=f32)
        act = (gate / (1.0 + jnp.exp(-gate)) * up).astype(bf16)
        product = jnp.dot(act, downs[origin], preferred_element_type=f32)
        wide[...] = product if k == 0 else wide[...] + product
    lanes = out.shape[2]
    left = lax.broadcasted_iota(jnp.int32, (half, lanes), 1) < lanes // 2
    for group in range(out.shape[0] // experts):
        for pair in range(experts // 2):
            cols = pl.ds(pair * lanes, lanes)
            at = 2 * group * padded
            low = wide[pl.ds(at, half), cols]
            high = wide[pl.ds(at + padded, half), cols]
            out[group * experts + 2 * pair] = jnp.where(left, low, pltpu.roll(high, lanes // 2, 1)).astype(bf16)
            out[group * experts + 2 * pair + 1] = jnp.where(
                left, pltpu.roll(low, lanes // 2, 1), high
            ).astype(bf16)


def combine_kernel(experts, half, padded, back, mid, slots, fixed, rows, out, table):
    table[...] = jnp.zeros_like(table)
    for e in range(experts):
        total = back[e].astype(f32)
        for copy in range(1, back.shape[0] // experts):
            total = total + back[copy * experts + e].astype(f32)
        table[pl.ds(e * padded, half), :] = total
    rounded = table[...].astype(bf16)
    feats = mid.shape[0]
    low = rows[...]
    total = mid[...].astype(f32)
    for k in range(slots.shape[0]):
        slot = slots[k : k + 1]
        picked = 0.0
        for at, begin in ((low, 0), (low + half, feats)):
            both = lax.dot_general(
                rounded, chosen(at, slot).astype(bf16), (((0,), (0,)), ((), ())), preferred_element_type=f32
            )
            picked = picked + both[begin : begin + feats]
        total = total + picked * (fixed[k : k + 1].astype(f32) * FIXED_SCALE)
    out[...] = total.astype(bf16)


def local_kernel(body, *out_shapes, scratch=()):
    return pl.pallas_call(
        body,
        out_shape=out_shapes,
        scratch_shapes=scratch,
        compiler_params=pltpu.CompilerParams(vmem_limit_bytes=40 * 1024 * 1024),
    )


def attention(queries, keys, values, local_frame, frame_rows):
    width = keys.shape[0]
    scale = 1.0 / math.sqrt(queries.shape[1])
    scores = lax.dot_general(queries, keys, (((1,), (1,)), ((), ())), preferred_element_type=f32) * scale
    column_frame = lax.broadcasted_iota(jnp.int32, (1, width), 1) // frame_rows
    inside = column_frame == local_frame[:, None]
    scores = jnp.where(inside, scores, MASKED_SCORE)
    row_max = jnp.max(scores, axis=1, keepdims=True)
    expon = jnp.exp(scores - row_max)
    row_total = jnp.sum(expon, axis=1, keepdims=True)
    probability = (expon / row_total).astype(bf16)
    mixed = jnp.dot(probability, values, preferred_element_type=f32)
    return jnp.where(local_frame[:, None] >= 0, mixed, 0.0).astype(bf16)


def per_device(
    hidden_in,
    queries,
    frame_keys,
    frame_values,
    cited_frame,
    frame_slot,
    attn_gate,
    out_weight,
    mlp_gain,
    expert_ids,
    gate_fixed,
    w_in,
    w_down,
):
    head = queries.shape[1]
    tokens = queries.shape[0]
    nx, nz, nh = lax.axis_size("x"), lax.axis_size("z"), lax.axis_size("yh")
    experts = lax.axis_size(EXP)
    near = lax.axis_size(NEAR)
    feats = hidden_in.shape[1]
    yh, x, z = lax.axis_index("yh"), lax.axis_index("x"), lax.axis_index("z")
    held, frame_rows = frame_keys.shape[0], frame_keys.shape[1]
    own = jnp.concatenate(
        [
            lax.dynamic_slice_in_dim(frame_keys, z * head, head, 2).reshape(held * frame_rows, head),
            lax.dynamic_slice_in_dim(frame_values, z * head, head, 2).reshape(held * frame_rows, head),
        ],
        axis=0,
    )
    frame_cols = lax.broadcasted_iota(jnp.int32, (tokens, frame_slot.shape[0]), 1)
    token_slot = jnp.sum(jnp.where(cited_frame[:, None] == frame_cols, frame_slot[None, :], 0), axis=1)
    slot_rows = jnp.zeros((16, head), bf16).at[: tokens // head].set(
        token_slot.reshape(tokens // head, head).astype(bf16)
    )
    packed, own = tie(jnp.concatenate([queries, slot_rows]), own)
    other = swap(own, "yh")
    down_all = lax.all_gather(w_down[0], "x")
    gathered = spread(packed, "x")
    gathered, wide_in = tie(gathered, w_in[0])
    turned = out_weight.T
    own_up = wide_in[:, 1]
    gate_all = lax.all_gather(wide_in[:, 0], "x")
    turned = turned.reshape(feats, nz, near * head).transpose(1, 0, 2)
    near_weight = lax.all_to_all(turned, "z", 0, 0, tiled=True).reshape(nz * feats, near * head)
    all_queries = gathered[:, :tokens].reshape(nx * tokens, head)
    all_slots = gathered[:, tokens : tokens + tokens // head].reshape(nx * tokens).astype(jnp.int32)
    own_frame = all_slots - held * (yh * nx + x)
    other_frame = all_slots - held * ((1 - yh) * nx + x)
    local_frame = jnp.where(
        (own_frame >= 0) & (own_frame < held),
        own_frame,
        jnp.where((other_frame >= 0) & (other_frame < held), other_frame + held, -1),
    )
    half = held * frame_rows
    keys = jnp.concatenate([own[:half], other[:half]], axis=0)
    values = jnp.concatenate([own[half:], other[half:]], axis=0)
    mixed = attention(all_queries, keys, values, local_frame, frame_rows)
    back = mixed.reshape(nx, tokens, head)
    attended = lax.dynamic_index_in_dim(back, x, 0, keepdims=False).astype(f32)
    for k in range(1, nx):
        piece = lax.dynamic_index_in_dim(back, (x + k) % nx, 0, keepdims=False)
        attended = attended + shift(piece, "x", k).astype(f32)
    attended, own_up = tie(attended.astype(bf16), own_up)
    left_up, right_up = shift(own_up, "x", 1), shift(own_up, "x", -1)
    heads = lax.all_gather(attended, NEAR, axis=1, tiled=True)
    partial = lax.dot_general(
        near_weight, heads, (((1,), (1,)), ((), ())), preferred_element_type=f32
    ).astype(bf16)
    partial, down_all = tie(partial, down_all)
    parts = lax.all_to_all(partial.reshape(nz, feats, tokens), "z", 0, 0, tiled=True)
    capacity = 6 * tokens // experts
    half, padded = capacity // 2, -(-(capacity // 2) // 8) * 8
    lanes = 2 * feats
    table = row_slots(experts, capacity, padded)
    slots = slots_of(expert_ids, capacity, experts)
    mid, sent = local_kernel(
        functools.partial(dispatch_kernel, experts, half, padded),
        jax.ShapeDtypeStruct((feats, tokens), bf16),
        jax.ShapeDtypeStruct((nh * experts, half, lanes), bf16),
    )(parts, hidden_in.T, attn_gate[:, None], slots, table)
    sent, left_up, right_up = tie(sent, left_up, right_up)
    cut = w_in.shape[1] // 2
    far_low, far_high = shift(left_up[:cut], "x", 1), shift(right_up[cut:], "x", -1)
    came = lax.all_to_all(sent, BOTH, 0, 0, tiled=True)
    rows = 2 * nh * padded
    (normed,) = local_kernel(
        functools.partial(assemble_kernel, experts, half, padded),
        jax.ShapeDtypeStruct((rows, experts * feats), bf16),
        scratch=(pltpu.VMEM((rows, experts * feats), f32),),
    )(came, mlp_gain[None])

    in_vmem = pl.BlockSpec(memory_space=pltpu.VMEM)
    dealt = pl.pallas_call(
        functools.partial(expert_kernel, experts, half, padded),
        in_specs=[pl.BlockSpec(memory_space=pltpu.SMEM)] + [in_vmem] * 8,
        out_specs=in_vmem,
        out_shape=jax.ShapeDtypeStruct(came.shape, bf16),
        scratch_shapes=[pltpu.VMEM((rows, experts * feats), f32)],
        compiler_params=pltpu.CompilerParams(vmem_limit_bytes=40 * 1024 * 1024),
    )(x[None], normed, gate_all, own_up, left_up, right_up, far_low, far_high, down_all)
    back_sums = lax.all_to_all(dealt, BOTH, 0, 0, tiled=True)
    (out,) = local_kernel(
        functools.partial(combine_kernel, experts, half, padded),
        jax.ShapeDtypeStruct((feats, tokens), bf16),
        scratch=(pltpu.VMEM((experts * padded, lanes), f32),),
    )(back_sums, mid, slots, gate_fixed.T, table)
    return out.T


def solution(mesh):
    fine = Mesh(mesh.devices.reshape(2, 4, 8, 4, 2), SEQ + EXP)
    return jax.shard_map(
        per_device,
        mesh=fine,
        in_specs=(
            P(SEQ, EXP),
            P(SEQ, EXP),
            P(SEQ, None, None),
            P(SEQ, None, None),
            P(SEQ),
            P(),
            P(EXP),
            P(None, EXP),
            P(),
            P(SEQ, None),
            P(SEQ, None),
            P(EXP, None, None, SEQ),
            P(EXP, SEQ, None),
        ),
        out_specs=P(SEQ, EXP),
        check_vma=False,
    )
```

```python
import functools
import math

import jax
import jax.numpy as jnp
import numpy as np
from jax import lax
from jax.experimental import pallas as pl
from jax.experimental.pallas import tpu as pltpu
from jax.sharding import Mesh
from jax.sharding import PartitionSpec as P

FIXED_SCALE = 1.0 / 65536.0
NORM_EPSILON = 1e-05
MASKED_SCORE = -1e30
SEQ = ("yh", "x")
EXP = ("z", "yl", "core")
NEAR = ("yl", "core")
BOTH = ("yh",) + EXP
f32, bf16 = jnp.float32, jnp.bfloat16


def swap(v, axis):
    return lax.ppermute(v, axis, [(0, 1), (1, 0)])


def shift(v, axis, by):
    n = lax.axis_size(axis)
    return lax.ppermute(v, axis, [(i, (i + by) % n) for i in range(n)])


def tie(*values):
    return lax.optimization_barrier(values)


def spread(v, axis):
    n = lax.axis_size(axis)
    return lax.all_to_all(jnp.broadcast_to(v[None], (n,) + v.shape), axis, 0, 0, tiled=True)


def slots_of(expert_ids, capacity, experts):
    token_count, top_count = expert_ids.shape
    flat_ids = expert_ids.reshape(-1)
    assigned = flat_ids.shape[0]
    expert_cols = lax.broadcasted_iota(jnp.int32, (assigned, experts), 1)
    matches = flat_ids[:, None] == expert_cols
    before = lax.broadcasted_iota(jnp.int32, (assigned, assigned), 1) < lax.broadcasted_iota(
        jnp.int32, (assigned, assigned), 0
    )
    counts = jnp.dot(before.astype(bf16), matches.astype(bf16), preferred_element_type=f32)
    rank_of = jnp.sum(jnp.where(matches, counts, 0.0), axis=1).astype(jnp.int32)
    return (flat_ids * capacity + rank_of).reshape(token_count, top_count).T


def row_slots(experts, capacity, padded):
    half = capacity // 2
    row = np.arange(experts * padded)
    at = row % padded
    return np.where(at < half, row // padded * capacity + at, -4 * capacity).astype(np.int32)[:, None]


def chosen(rows, slot):
    return jnp.where(rows == slot, 1.0, 0.0)


def dispatch_kernel(experts, half, padded, parts, hidden, gate, slots, rows, mid_out, sent):
    summed = jnp.sum(parts[...].astype(f32), axis=0)
    mid = (hidden[...].astype(f32) + jnp.tanh(gate[...]) * summed).astype(bf16)
    mid_out[...] = mid
    nothing = jnp.zeros_like(mid)
    low = rows[...]
    first, second = slots[0:1], slots[1:2]
    total = 0.0
    for at, wide in ((low, (mid, nothing)), (low + half, (nothing, mid))):
        pick = (chosen(at, first) + chosen(at, second)).astype(bf16)
        total = total + lax.dot_general(
            pick, jnp.concatenate(wide, axis=0), (((1,), (1,)), ((), ())), preferred_element_type=f32
        )
    for e in range(experts):
        block = total[e * padded : e * padded + half].astype(bf16)
        for copy in range(sent.shape[0] // experts):
            sent[copy * experts + e] = block


def assemble_kernel(experts, half, padded, came, gain, normed, wide):
    wide[...] = jnp.zeros_like(wide)
    lanes = came.shape[2]
    left = lax.broadcasted_iota(jnp.int32, (half, lanes), 1) < lanes // 2
    for group in range(came.shape[0] // experts):
        for pair in range(experts // 2):
            one = came[group * experts + 2 * pair].astype(f32)
            two = came[group * experts + 2 * pair + 1].astype(f32)
            cols = pl.ds(pair * lanes, lanes)
            at = 2 * group * padded
            wide[pl.ds(at, half), cols] = jnp.where(left, one, pltpu.roll(two, lanes // 2, 1))
            wide[pl.ds(at + padded, half), cols] = jnp.where(left, pltpu.roll(one, lanes // 2, 1), two)
    rows = wide[...]
    mean_square = jnp.mean(rows * rows, axis=1, keepdims=True)
    normed[...] = (rows * lax.rsqrt(mean_square + NORM_EPSILON) * gain[...]).astype(bf16)


def expert_kernel(
    experts,
    half,
    padded,
    place,
    normed,
    own_up,
    left_up,
    right_up,
    far_low,
    far_high,
    gates_there,
    downs_there,
    out,
    wide,
    gates,
    downs,
    gate_sems,
    down_sems,
):
    nx = downs.shape[0]
    origins = [(place[0] + turn) % nx for turn in (0, nx - 1, 1, 2)]
    gate_copies = [
        pltpu.make_async_copy(gates_there.at[origin], gates.at[k], gate_sems.at[k])
        for k, origin in enumerate(origins)
    ]
    down_copies = [
        pltpu.make_async_copy(downs_there.at[origin], downs.at[k], down_sems.at[k])
        for k, origin in enumerate(origins)
    ]
    for gate_copy, down_copy in zip(gate_copies, down_copies):
        gate_copy.start()
        down_copy.start()
    rows = normed[...]
    cut = far_low.shape[0]
    for k, ups in enumerate(((own_up,), (left_up,), (right_up,), (far_low, far_high))):
        gate_copies[k].wait()
        gate = jnp.dot(rows, gates[k], preferred_element_type=f32)
        if len(ups) == 1:
            up = jnp.dot(rows, ups[0][...], preferred_element_type=f32)
        else:
            up = jnp.dot(rows[:, :cut], ups[0][...], preferred_element_type=f32)
            up = up + jnp.dot(rows[:, cut:], ups[1][...], preferred_element_type=f32)
        act = (gate / (1.0 + jnp.exp(-gate)) * up).astype(bf16)
        down_copies[k].wait()
        product = jnp.dot(act, downs[k], preferred_element_type=f32)
        wide[...] = product if k == 0 else wide[...] + product
    lanes = out.shape[2]
    left = lax.broadcasted_iota(jnp.int32, (half, lanes), 1) < lanes // 2
    for group in range(out.shape[0] // experts):
        for pair in range(experts // 2):
            cols = pl.ds(pair * lanes, lanes)
            at = 2 * group * padded
            low = wide[pl.ds(at, half), cols]
            high = wide[pl.ds(at + padded, half), cols]
            out[group * experts + 2 * pair] = jnp.where(left, low, pltpu.roll(high, lanes // 2, 1)).astype(bf16)
            out[group * experts + 2 * pair + 1] = jnp.where(
                left, pltpu.roll(low, lanes // 2, 1), high
            ).astype(bf16)


def combine_kernel(experts, half, padded, back, mid, slots, fixed, rows, out, table):
    table[...] = jnp.zeros_like(table)
    for e in range(experts):
        total = back[e].astype(f32)
        for copy in range(1, back.shape[0] // experts):
            total = total + back[copy * experts + e].astype(f32)
        table[pl.ds(e * padded, half), :] = total
    rounded = table[...].astype(bf16)
    feats = mid.shape[0]
    low = rows[...]
    total = mid[...].astype(f32)
    for k in range(slots.shape[0]):
        slot = slots[k : k + 1]
        picked = 0.0
        for at, begin in ((low, 0), (low + half, feats)):
            both = lax.dot_general(
                rounded, chosen(at, slot).astype(bf16), (((0,), (0,)), ((), ())), preferred_element_type=f32
            )
            picked = picked + both[begin : begin + feats]
        total = total + picked * (fixed[k : k + 1].astype(f32) * FIXED_SCALE)
    out[...] = total.astype(bf16)


def local_kernel(body, *out_shapes, scratch=()):
    return pl.pallas_call(
        body,
        out_shape=out_shapes,
        scratch_shapes=scratch,
        compiler_params=pltpu.CompilerParams(vmem_limit_bytes=40 * 1024 * 1024),
    )


def attention(queries, keys, values, local_frame, frame_rows):
    width = keys.shape[0]
    scale = 1.0 / math.sqrt(queries.shape[1])
    scores = lax.dot_general(queries, keys, (((1,), (1,)), ((), ())), preferred_element_type=f32) * scale
    column_frame = lax.broadcasted_iota(jnp.int32, (1, width), 1) // frame_rows
    inside = column_frame == local_frame[:, None]
    scores = jnp.where(inside, scores, MASKED_SCORE)
    row_max = jnp.max(scores, axis=1, keepdims=True)
    expon = jnp.exp(scores - row_max)
    row_total = jnp.sum(expon, axis=1, keepdims=True)
    probability = (expon / row_total).astype(bf16)
    mixed = jnp.dot(probability, values, preferred_element_type=f32)
    return jnp.where(local_frame[:, None] >= 0, mixed, 0.0).astype(bf16)


def per_device(
    hidden_in,
    queries,
    frame_keys,
    frame_values,
    cited_frame,
    frame_slot,
    attn_gate,
    out_weight,
    mlp_gain,
    expert_ids,
    gate_fixed,
    w_in,
    w_down,
):
    head = queries.shape[1]
    tokens = queries.shape[0]
    nx, nz, nh = lax.axis_size("x"), lax.axis_size("z"), lax.axis_size("yh")
    experts = lax.axis_size(EXP)
    near = lax.axis_size(NEAR)
    feats = hidden_in.shape[1]
    yh, x, z = lax.axis_index("yh"), lax.axis_index("x"), lax.axis_index("z")
    held, frame_rows = frame_keys.shape[0], frame_keys.shape[1]
    own = jnp.concatenate(
        [
            lax.dynamic_slice_in_dim(frame_keys, z * head, head, 2).reshape(held * frame_rows, head),
            lax.dynamic_slice_in_dim(frame_values, z * head, head, 2).reshape(held * frame_rows, head),
        ],
        axis=0,
    )
    frame_cols = lax.broadcasted_iota(jnp.int32, (tokens, frame_slot.shape[0]), 1)
    token_slot = jnp.sum(jnp.where(cited_frame[:, None] == frame_cols, frame_slot[None, :], 0), axis=1)
    slot_rows = jnp.zeros((16, head), bf16).at[: tokens // head].set(
        token_slot.reshape(tokens // head, head).astype(bf16)
    )
    packed, own = tie(jnp.concatenate([queries, slot_rows]), own)
    other = swap(own, "yh")
    down_all = lax.all_gather(w_down[0], "x")
    gathered = spread(packed, "x")
    wide_in = w_in[0]
    turned = out_weight.T
    own_up = wide_in[:, 1]
    gate_all = lax.all_gather(wide_in[:, 0], "x")
    turned = turned.reshape(feats, nz, near * head).transpose(1, 0, 2)
    near_weight = lax.all_to_all(turned, "z", 0, 0, tiled=True).reshape(nz * feats, near * head)
    all_queries = gathered[:, :tokens].reshape(nx * tokens, head)
    all_slots = gathered[:, tokens : tokens + tokens // head].reshape(nx * tokens).astype(jnp.int32)
    own_frame = all_slots - held * (yh * nx + x)
    other_frame = all_slots - held * ((1 - yh) * nx + x)
    local_frame = jnp.where(
        (own_frame >= 0) & (own_frame < held),
        own_frame,
        jnp.where((other_frame >= 0) & (other_frame < held), other_frame + held, -1),
    )
    half = held * frame_rows
    keys = jnp.concatenate([own[:half], other[:half]], axis=0)
    values = jnp.concatenate([own[half:], other[half:]], axis=0)
    mixed = attention(all_queries, keys, values, local_frame, frame_rows)
    back = mixed.reshape(nx, tokens, head)
    pieces = [
        shift(lax.dynamic_index_in_dim(back, (x + k) % nx, 0, keepdims=False), "x", k) for k in range(1, nx)
    ]
    pieces[0], own_up = tie(pieces[0], own_up)
    left_up, right_up = shift(own_up, "x", 1), shift(own_up, "x", -1)
    attended = sum(
        piece.astype(f32) for piece in [lax.dynamic_index_in_dim(back, x, 0, keepdims=False)] + pieces
    ).astype(bf16)
    heads = lax.all_gather(attended, NEAR, axis=1, tiled=True)
    partial = lax.dot_general(
        near_weight, heads, (((1,), (1,)), ((), ())), preferred_element_type=f32
    ).astype(bf16)
    partial, down_all = tie(partial, down_all)
    parts = lax.all_to_all(partial.reshape(nz, feats, tokens), "z", 0, 0, tiled=True)
    capacity = 6 * tokens // experts
    half, padded = capacity // 2, -(-(capacity // 2) // 8) * 8
    lanes = 2 * feats
    table = row_slots(experts, capacity, padded)
    slots = slots_of(expert_ids, capacity, experts)
    mid, sent = local_kernel(
        functools.partial(dispatch_kernel, experts, half, padded),
        jax.ShapeDtypeStruct((feats, tokens), bf16),
        jax.ShapeDtypeStruct((nh * experts, half, lanes), bf16),
    )(parts, hidden_in.T, attn_gate[:, None], slots, table)
    sent, left_up, right_up = tie(sent, left_up, right_up)
    cut = w_in.shape[1] // 2
    far_low, far_high = shift(left_up[:cut], "x", 1), shift(right_up[cut:], "x", -1)
    came = lax.all_to_all(sent, BOTH, 0, 0, tiled=True)
    rows = 2 * nh * padded
    (normed,) = local_kernel(
        functools.partial(assemble_kernel, experts, half, padded),
        jax.ShapeDtypeStruct((rows, experts * feats), bf16),
        scratch=(pltpu.VMEM((rows, experts * feats), f32),),
    )(came, mlp_gain[None])

    in_vmem = pl.BlockSpec(memory_space=pltpu.VMEM)
    dealt = pl.pallas_call(
        functools.partial(expert_kernel, experts, half, padded),
        in_specs=[pl.BlockSpec(memory_space=pltpu.SMEM)] + [in_vmem] * 6 + [pl.BlockSpec(memory_space=pl.ANY)] * 2,
        out_specs=in_vmem,
        out_shape=jax.ShapeDtypeStruct(came.shape, bf16),
        scratch_shapes=[
            pltpu.VMEM((rows, experts * feats), f32),
            pltpu.VMEM(gate_all.shape, bf16),
            pltpu.VMEM(down_all.shape, bf16),
            pltpu.SemaphoreType.DMA((nx,)),
            pltpu.SemaphoreType.DMA((nx,)),
        ],
        compiler_params=pltpu.CompilerParams(vmem_limit_bytes=40 * 1024 * 1024),
    )(x[None], normed, own_up, left_up, right_up, far_low, far_high, gate_all, down_all)
    back_sums = lax.all_to_all(dealt, BOTH, 0, 0, tiled=True)
    (out,) = local_kernel(
        functools.partial(combine_kernel, experts, half, padded),
        jax.ShapeDtypeStruct((feats, tokens), bf16),
        scratch=(pltpu.VMEM((experts * padded, lanes), f32),),
    )(back_sums, mid, slots, gate_fixed.T, table)
    return out.T


def solution(mesh):
    fine = Mesh(mesh.devices.reshape(2, 4, 8, 4, 2), SEQ + EXP)
    return jax.shard_map(
        per_device,
        mesh=fine,
        in_specs=(
            P(SEQ, EXP),
            P(SEQ, EXP),
            P(SEQ, None, None),
            P(SEQ, None, None),
            P(SEQ),
            P(),
            P(EXP),
            P(None, EXP),
            P(),
            P(SEQ, None),
            P(SEQ, None),
            P(EXP, None, None, SEQ),
            P(EXP, SEQ, None),
        ),
        out_specs=P(SEQ, EXP),
        check_vma=False,
    )
```

```python
import functools
import math

import jax
import jax.numpy as jnp
import numpy as np
from jax import lax
from jax.experimental import pallas as pl
from jax.experimental.pallas import tpu as pltpu
from jax.sharding import Mesh
from jax.sharding import PartitionSpec as P

FIXED_SCALE = 1.0 / 65536.0
NORM_EPSILON = 1e-05
MASKED_SCORE = -1e30
SEQ = ("yh", "x")
EXP = ("z", "yl", "core")
NEAR = ("yl", "core")
BOTH = ("yh",) + EXP
f32, bf16 = jnp.float32, jnp.bfloat16


def swap(v, axis):
    return lax.ppermute(v, axis, [(0, 1), (1, 0)])


def shift(v, axis, by):
    n = lax.axis_size(axis)
    return lax.ppermute(v, axis, [(i, (i + by) % n) for i in range(n)])


def tie(*values):
    return lax.optimization_barrier(values)


def spread(v, axis):
    n = lax.axis_size(axis)
    return lax.all_to_all(jnp.broadcast_to(v[None], (n,) + v.shape), axis, 0, 0, tiled=True)


def slots_of(expert_ids, capacity, experts):
    token_count, top_count = expert_ids.shape
    flat_ids = expert_ids.reshape(-1)
    assigned = flat_ids.shape[0]
    expert_cols = lax.broadcasted_iota(jnp.int32, (assigned, experts), 1)
    matches = flat_ids[:, None] == expert_cols
    before = lax.broadcasted_iota(jnp.int32, (assigned, assigned), 1) < lax.broadcasted_iota(
        jnp.int32, (assigned, assigned), 0
    )
    counts = jnp.dot(before.astype(bf16), matches.astype(bf16), preferred_element_type=f32)
    rank_of = jnp.sum(jnp.where(matches, counts, 0.0), axis=1).astype(jnp.int32)
    return (flat_ids * capacity + rank_of).reshape(token_count, top_count).T


def row_slots(experts, capacity, padded):
    half = capacity // 2
    row = np.arange(experts * padded)
    at = row % padded
    return np.where(at < half, row // padded * capacity + at, -4 * capacity).astype(np.int32)[:, None]


def chosen(rows, slot):
    return jnp.where(rows == slot, 1.0, 0.0)


def dispatch_kernel(experts, half, padded, parts, hidden, gate, slots, rows, mid_out, sent):
    summed = jnp.sum(parts[...].astype(f32), axis=0)
    mid = (hidden[...].astype(f32) + jnp.tanh(gate[...]) * summed).astype(bf16)
    mid_out[...] = mid
    nothing = jnp.zeros_like(mid)
    low = rows[...]
    first, second = slots[0:1], slots[1:2]
    total = 0.0
    for at, wide in ((low, (mid, nothing)), (low + half, (nothing, mid))):
        pick = (chosen(at, first) + chosen(at, second)).astype(bf16)
        total = total + lax.dot_general(
            pick, jnp.concatenate(wide, axis=0), (((1,), (1,)), ((), ())), preferred_element_type=f32
        )
    for e in range(experts):
        block = total[e * padded : e * padded + half].astype(bf16)
        for copy in range(sent.shape[0] // experts):
            sent[copy * experts + e] = block


def assemble_kernel(experts, half, padded, came, gain, normed, wide):
    wide[...] = jnp.zeros_like(wide)
    lanes = came.shape[2]
    left = lax.broadcasted_iota(jnp.int32, (half, lanes), 1) < lanes // 2
    for group in range(came.shape[0] // experts):
        for pair in range(experts // 2):
            one = came[group * experts + 2 * pair].astype(f32)
            two = came[group * experts + 2 * pair + 1].astype(f32)
            cols = pl.ds(pair * lanes, lanes)
            at = 2 * group * padded
            wide[pl.ds(at, half), cols] = jnp.where(left, one, pltpu.roll(two, lanes // 2, 1))
            wide[pl.ds(at + padded, half), cols] = jnp.where(left, pltpu.roll(one, lanes // 2, 1), two)
    rows = wide[...]
    mean_square = jnp.mean(rows * rows, axis=1, keepdims=True)
    normed[...] = (rows * lax.rsqrt(mean_square + NORM_EPSILON) * gain[...]).astype(bf16)


def expert_kernel(
    experts,
    half,
    padded,
    place,
    normed,
    own_up,
    left_up,
    right_up,
    far_low,
    far_high,
    gates_there,
    downs_there,
    out,
    wide,
    gates,
    downs,
    gate_sems,
    down_sems,
):
    nx = downs.shape[0]
    origins = [(place[0] + turn) % nx for turn in (0, nx - 1, 1, 2)]
    gate_copies = [
        pltpu.make_async_copy(gates_there.at[origin], gates.at[k], gate_sems.at[k])
        for k, origin in enumerate(origins)
    ]
    down_copies = [
        pltpu.make_async_copy(downs_there.at[origin], downs.at[k], down_sems.at[k])
        for k, origin in enumerate(origins)
    ]
    for gate_copy, down_copy in zip(gate_copies, down_copies):
        gate_copy.start()
        down_copy.start()
    rows = normed[...]
    cut = far_low.shape[0]
    for k, ups in enumerate(((own_up,), (left_up,), (right_up,), (far_low, far_high))):
        gate_copies[k].wait()
        gate = jnp.dot(rows, gates[k], preferred_element_type=f32)
        if len(ups) == 1:
            up = jnp.dot(rows, ups[0][...], preferred_element_type=f32)
        else:
            up = jnp.dot(rows[:, :cut], ups[0][...], preferred_element_type=f32)
            up = up + jnp.dot(rows[:, cut:], ups[1][...], preferred_element_type=f32)
        act = (gate / (1.0 + jnp.exp(-gate)) * up).astype(bf16)
        down_copies[k].wait()
        product = jnp.dot(act, downs[k], preferred_element_type=f32)
        wide[...] = product if k == 0 else wide[...] + product
    lanes = out.shape[2]
    left = lax.broadcasted_iota(jnp.int32, (half, lanes), 1) < lanes // 2
    for group in range(out.shape[0] // experts):
        for pair in range(experts // 2):
            cols = pl.ds(pair * lanes, lanes)
            at = 2 * group * padded
            low = wide[pl.ds(at, half), cols]
            high = wide[pl.ds(at + padded, half), cols]
            out[group * experts + 2 * pair] = jnp.where(left, low, pltpu.roll(high, lanes // 2, 1)).astype(bf16)
            out[group * experts + 2 * pair + 1] = jnp.where(
                left, pltpu.roll(low, lanes // 2, 1), high
            ).astype(bf16)


def combine_kernel(experts, half, padded, back, mid, slots, fixed, rows, out, table):
    table[...] = jnp.zeros_like(table)
    for e in range(experts):
        total = back[e].astype(f32)
        for copy in range(1, back.shape[0] // experts):
            total = total + back[copy * experts + e].astype(f32)
        table[pl.ds(e * padded, half), :] = total
    rounded = table[...].astype(bf16)
    feats = mid.shape[0]
    low = rows[...]
    total = mid[...].astype(f32)
    for k in range(slots.shape[0]):
        slot = slots[k : k + 1]
        picked = 0.0
        for at, begin in ((low, 0), (low + half, feats)):
            both = lax.dot_general(
                rounded, chosen(at, slot).astype(bf16), (((0,), (0,)), ((), ())), preferred_element_type=f32
            )
            picked = picked + both[begin : begin + feats]
        total = total + picked * (fixed[k : k + 1].astype(f32) * FIXED_SCALE)
    out[...] = total.astype(bf16)


def local_kernel(body, *out_shapes, scratch=()):
    return pl.pallas_call(
        body,
        out_shape=out_shapes,
        scratch_shapes=scratch,
        compiler_params=pltpu.CompilerParams(vmem_limit_bytes=40 * 1024 * 1024),
    )


def attention(queries, keys, values, local_frame, frame_rows):
    width = keys.shape[0]
    scale = 1.0 / math.sqrt(queries.shape[1])
    scores = lax.dot_general(queries, keys, (((1,), (1,)), ((), ())), preferred_element_type=f32) * scale
    column_frame = lax.broadcasted_iota(jnp.int32, (1, width), 1) // frame_rows
    inside = column_frame == local_frame[:, None]
    scores = jnp.where(inside, scores, MASKED_SCORE)
    row_max = jnp.max(scores, axis=1, keepdims=True)
    expon = jnp.exp(scores - row_max)
    row_total = jnp.sum(expon, axis=1, keepdims=True)
    probability = (expon / row_total).astype(bf16)
    mixed = jnp.dot(probability, values, preferred_element_type=f32)
    return jnp.where(local_frame[:, None] >= 0, mixed, 0.0).astype(bf16)


def per_device(
    hidden_in,
    queries,
    frame_keys,
    frame_values,
    cited_frame,
    frame_slot,
    attn_gate,
    out_weight,
    mlp_gain,
    expert_ids,
    gate_fixed,
    w_in,
    w_down,
):
    head = queries.shape[1]
    tokens = queries.shape[0]
    nx, nz, nh = lax.axis_size("x"), lax.axis_size("z"), lax.axis_size("yh")
    experts = lax.axis_size(EXP)
    near = lax.axis_size(NEAR)
    feats = hidden_in.shape[1]
    yh, x, z = lax.axis_index("yh"), lax.axis_index("x"), lax.axis_index("z")
    held, frame_rows = frame_keys.shape[0], frame_keys.shape[1]
    own = jnp.concatenate(
        [
            lax.dynamic_slice_in_dim(frame_keys, z * head, head, 2).reshape(held * frame_rows, head),
            lax.dynamic_slice_in_dim(frame_values, z * head, head, 2).reshape(held * frame_rows, head),
        ],
        axis=0,
    )
    frame_cols = lax.broadcasted_iota(jnp.int32, (tokens, frame_slot.shape[0]), 1)
    token_slot = jnp.sum(jnp.where(cited_frame[:, None] == frame_cols, frame_slot[None, :], 0), axis=1)
    slot_rows = jnp.zeros((16, head), bf16).at[: tokens // head].set(
        token_slot.reshape(tokens // head, head).astype(bf16)
    )
    packed, own = tie(jnp.concatenate([queries, slot_rows]), own)
    other = swap(own, "yh")
    down_all = lax.all_gather(w_down[0], "x")
    gathered = spread(packed, "x")
    wide_in = w_in[0]
    turned = out_weight.T
    own_up = wide_in[:, 1]
    gate_all = lax.all_gather(wide_in[:, 0], "x")
    turned = turned.reshape(feats, nz, near * head).transpose(1, 0, 2)
    near_weight = lax.all_to_all(turned, "z", 0, 0, tiled=True).reshape(nz * feats, near * head)
    all_queries = gathered[:, :tokens].reshape(nx * tokens, head)
    all_slots = gathered[:, tokens : tokens + tokens // head].reshape(nx * tokens).astype(jnp.int32)
    own_frame = all_slots - held * (yh * nx + x)
    other_frame = all_slots - held * ((1 - yh) * nx + x)
    local_frame = jnp.where(
        (own_frame >= 0) & (own_frame < held),
        own_frame,
        jnp.where((other_frame >= 0) & (other_frame < held), other_frame + held, -1),
    )
    half = held * frame_rows
    keys = jnp.concatenate([own[:half], other[:half]], axis=0)
    values = jnp.concatenate([own[half:], other[half:]], axis=0)
    mixed = attention(all_queries, keys, values, local_frame, frame_rows)
    back = mixed.reshape(nx, tokens, head)
    pieces = [
        shift(lax.dynamic_index_in_dim(back, (x + k) % nx, 0, keepdims=False), "x", k) for k in range(1, nx)
    ]
    pieces[0], own_up = tie(pieces[0], own_up)
    left_up, right_up = shift(own_up, "x", 1), shift(own_up, "x", -1)
    attended = sum(
        piece.astype(f32) for piece in [lax.dynamic_index_in_dim(back, x, 0, keepdims=False)] + pieces
    ).astype(bf16)
    heads = lax.all_gather(attended, NEAR, axis=1, tiled=True)
    partial = lax.dot_general(
        near_weight, heads, (((1,), (1,)), ((), ())), preferred_element_type=f32
    ).astype(bf16)
    partial, down_all = tie(partial, down_all)
    parts = lax.all_to_all(partial.reshape(nz, feats, tokens), "z", 0, 0, tiled=True)
    capacity = 6 * tokens // experts
    half, padded = capacity // 2, -(-(capacity // 2) // 8) * 8
    lanes = 2 * feats
    table = row_slots(experts, capacity, padded)
    slots = slots_of(expert_ids, capacity, experts)
    mid, sent = local_kernel(
        functools.partial(dispatch_kernel, experts, half, padded),
        jax.ShapeDtypeStruct((feats, tokens), bf16),
        jax.ShapeDtypeStruct((nh * experts, half, lanes), bf16),
    )(parts, hidden_in.T, attn_gate[:, None], slots, table)
    sent, left_up, right_up = tie(sent, left_up, right_up)
    cut = w_in.shape[1] // 2
    far_low, far_high = shift(left_up[:cut], "x", 1), shift(right_up[cut:], "x", -1)
    came = lax.all_to_all(sent, BOTH, 0, 0, tiled=True)
    rows = 2 * nh * padded
    (normed,) = local_kernel(
        functools.partial(assemble_kernel, experts, half, padded),
        jax.ShapeDtypeStruct((rows, experts * feats), bf16),
        scratch=(pltpu.VMEM((rows, experts * feats), f32),),
    )(came, mlp_gain[None])

    in_vmem = pl.BlockSpec(memory_space=pltpu.VMEM)
    dealt = pl.pallas_call(
        functools.partial(expert_kernel, experts, half, padded),
        in_specs=[pl.BlockSpec(memory_space=pltpu.SMEM)] + [in_vmem] * 6 + [pl.BlockSpec(memory_space=pl.ANY)] * 2,
        out_specs=in_vmem,
        out_shape=jax.ShapeDtypeStruct(came.shape, bf16),
        scratch_shapes=[
            pltpu.VMEM((rows, experts * feats), f32),
            pltpu.VMEM(gate_all.shape, bf16),
            pltpu.VMEM(down_all.shape, bf16),
            pltpu.SemaphoreType.DMA((nx,)),
            pltpu.SemaphoreType.DMA((nx,)),
        ],
        compiler_params=pltpu.CompilerParams(vmem_limit_bytes=48 * 1024 * 1024),
    )(x[None], normed, own_up, left_up, right_up, far_low, far_high, gate_all, down_all)
    back_sums = lax.all_to_all(dealt, BOTH, 0, 0, tiled=True)
    (out,) = local_kernel(
        functools.partial(combine_kernel, experts, half, padded),
        jax.ShapeDtypeStruct((feats, tokens), bf16),
        scratch=(pltpu.VMEM((experts * padded, lanes), f32),),
    )(back_sums, mid, slots, gate_fixed.T, table)
    return out.T


def solution(mesh):
    fine = Mesh(mesh.devices.reshape(2, 4, 8, 4, 2), SEQ + EXP)
    return jax.shard_map(
        per_device,
        mesh=fine,
        in_specs=(
            P(SEQ, EXP),
            P(SEQ, EXP),
            P(SEQ, None, None),
            P(SEQ, None, None),
            P(SEQ),
            P(),
            P(EXP),
            P(None, EXP),
            P(),
            P(SEQ, None),
            P(SEQ, None),
            P(EXP, None, None, SEQ),
            P(EXP, SEQ, None),
        ),
        out_specs=P(SEQ, EXP),
        check_vma=False,
    )
```
